128 devices in a mesh: role: 2 (over z_lo), fsdp: 64 (over z_hi, x, y, core).
Axes of the slice: x: 4, y: 4, z: 4 (z_hi: 2, z_lo: 2; z = z_hi * 2 + z_lo), core: 2. Of those that a mesh axis runs over, the one named last changes fastest.
Arguments:
- queries: bfloat16 [256, 2, 4096], P('fsdp'), may hold values from -504 to 504, as said below
- new_keys: bfloat16 [256, 2, 2048], P('fsdp'), may hold values from -9 to 9
- new_values: bfloat16 [256, 2, 2048], P('fsdp'), may hold values from -6 to 6
- cache_keys: bfloat16 [256, 256, 2048], P('fsdp'), may hold values from -9 to 9
- cache_values: bfloat16 [256, 256, 2048], P('fsdp'), may hold values from -6 to 6
- context_lengths: int32 [256], P('fsdp'), may hold values from 32 to 256
- rollout_rows: bfloat16 [512, 4, 5376], P(('role', 'fsdp')), may hold values from -6 to 6
- cotangents: bfloat16 [512, 4, 5376], P(('role', 'fsdp')), may hold values from -6 to 6
- rewards: float32 [512], P(('role', 'fsdp')), may hold values from 0 to 4
- prompt_keys: int32 [512], P(('role', 'fsdp')), may hold values from 0 to 7, as said below
- completion_lengths: int32 [512], P(('role', 'fsdp')), may hold values from 1 to 4
- finished_counts: int32 [128], P(('role', 'fsdp')), may hold values from 0 to 4, as said below
- gate_weight: bfloat16 [5376, 21504], P(None, 'fsdp'), may hold values from -0.078125 to 0.078125
- up_weight: bfloat16 [5376, 21504], P(None, 'fsdp'), may hold values from -0.078125 to 0.078125
- down_weight: bfloat16 [21504, 5376], P('fsdp'), may hold values from -0.0390625 to 0.0390625
Outputs:
- attended: bfloat16 [256, 2, 4096], P('fsdp')
- grad_gate: bfloat16 [5376, 21504], P('role', 'fsdp')
- grad_up: bfloat16 [5376, 21504], P('role', 'fsdp')
- grad_down: bfloat16 [21504, 5376], P('fsdp', 'role')
The draws below stay inside these ranges and needn't reach their ends.
Inputs may be any that keep to these rules, and one draw needn't show every extreme that they name: `queries`: in the shown draw these are plain normal numbers; the array's values stay within the range below. `finished_counts`: the first 64 entries belong to the generator devices and add up to 128; the last 64 entries, those of the learner devices, are zero. A device's live slots are its first ones. `prompt_keys`: over all live slots every prompt group is named by exactly 16 samples.
All inputs are finite; a program needn't handle non-finite values.
Results may differ from the reference program's by a relative error of at most 0.0058.
Values may be sent and summed in bfloat16 or wider, within the bound.
A program may use at most 192 MiB of HBM per device.

```python
import jax
import jax.numpy as jnp
from jax import lax

D = 5376
FF = 21504
HEADS = 32
KV_HEADS = 16
HEAD_DIM = 128
QSCALAR = 168
GROUP = 16
CL = 256
SLOTS = 4
SEQ = 4
SAMPLES = 256
GROUPS = 8
N_FSDP = 64


def rollout_layout(key):
    key = jax.random.fold_in(key, 11)
    order_key, fill_key, force_key, label_key, spare_key = jax.random.split(key, 5)
    half_count = N_FSDP // 2
    first_share = jax.random.randint(fill_key, (half_count,), 0, SLOTS + 1)
    forced = jax.random.randint(force_key, (), 0, half_count)
    first_share = jnp.where(jnp.arange(half_count) == forced, SLOTS, first_share)
    paired = jnp.stack([first_share, SLOTS - first_share], axis=1).reshape(-1)
    counts = paired[jax.random.permutation(order_key, N_FSDP)]
    live_slot = (jnp.arange(SLOTS)[None, :] < counts[:, None]).reshape(-1)
    ranking = jnp.cumsum(live_slot.astype(jnp.int32)) - 1
    labels = jax.random.permutation(label_key, GROUPS * GROUP) // GROUP
    chosen_label = labels[jnp.clip(ranking, 0, GROUPS * GROUP - 1)]
    spare_keys = jax.random.randint(spare_key, (2 * N_FSDP * SLOTS,), 0, GROUPS)
    generator_keys = jnp.where(live_slot, chosen_label, spare_keys[:N_FSDP * SLOTS])
    all_keys = jnp.concatenate([generator_keys, spare_keys[N_FSDP * SLOTS:]])
    all_counts = jnp.concatenate([counts, jnp.zeros((N_FSDP,), jnp.int32)])
    return (all_counts.astype(jnp.int32), all_keys.astype(jnp.int32))


def draw_finished_counts(key, part):
    return rollout_layout(key)[0]


def draw_prompt_keys(key, part):
    return rollout_layout(key)[1]


def draw_context_lengths(key, part):
    key = jax.random.fold_in(key, 3)
    length_key, index_key = jax.random.split(key)
    lengths = jax.random.randint(length_key, (SAMPLES,), CL // 8, CL + 1)
    forced_index = jax.random.randint(index_key, (), 0, SAMPLES)
    return jnp.where(jnp.arange(SAMPLES) == forced_index, CL, lengths).astype(jnp.int32)


def draw_queries(key, part):
    drawn_draw = jnp.clip(jax.random.normal(jax.random.fold_in(key, 5), (SAMPLES, 2, HEADS * HEAD_DIM), jnp.float32), -6.0, 6.0)
    return drawn_draw.astype(jnp.bfloat16)


def draw_cache_keys(key, part):
    drawn_draw = jnp.clip(1.5 * jax.random.normal(jax.random.fold_in(key, 7), (SAMPLES, CL, KV_HEADS * HEAD_DIM), jnp.float32), -9.0, 9.0)
    return drawn_draw.astype(jnp.bfloat16)


def place_ends(array, key, least, largest):
    place = [jax.random.randint(jax.random.fold_in(key, axis), (), 0, length) for axis, length in enumerate(array.shape)]
    widest = array.shape.index(max(array.shape))
    neighbour = place[:widest] + [(place[widest] + 1) % array.shape[widest]] + place[widest + 1:]
    return array.at[tuple(place)].set(least).at[tuple(neighbour)].set(largest)


def block_levels(key, shape, cuts, low, high):
    loudness = 1.0
    for axis_at, parts in cuts:
        draws = jax.random.uniform(jax.random.fold_in(jax.random.fold_in(key, 6), axis_at), (parts,), jnp.float32, low / len(cuts), high / len(cuts))
        loudness = loudness * jnp.repeat(jnp.exp(draws), shape[axis_at] // parts).reshape((-1,) + (1,) * (len(shape) - 1 - axis_at))
    return loudness


def scatter_about(rng, extent, scale, reach, pieces=(), dtype=jnp.bfloat16):
    drawn = jax.random.normal(rng, extent, jnp.float32) * scale
    if len(pieces) > 0:
        drawn = block_levels(rng, extent, pieces, -0.22, 0.18) * drawn
    return jnp.clip(drawn, min=-reach, max=reach).astype(dtype)


def setup_inputs(seed: int = 0) -> dict:
    splits = jax.random.split(jax.random.key(seed), 16)
    return {
        "queries": draw_queries(jax.random.fold_in(splits[15], 71), 0),
        "new_keys": scatter_about(splits[1], (SAMPLES, 2, KV_HEADS * HEAD_DIM), 1.5, 9.0, ((0, 64),)),
        "new_values": scatter_about(splits[2], (SAMPLES, 2, KV_HEADS * HEAD_DIM), 1.0, 6.0, ((0, 64),)),
        "cache_keys": draw_cache_keys(jax.random.fold_in(splits[15], 71), 0),
        "cache_values": scatter_about(splits[4], (SAMPLES, CL, KV_HEADS * HEAD_DIM), 1.0, 6.0, ((0, 64),)),
        "context_lengths": draw_context_lengths(jax.random.fold_in(splits[15], 71), 0),
        "rollout_rows": scatter_about(splits[6], (2 * N_FSDP * SLOTS, SEQ, D), 1.0, 6.0, ((0, 128),)),
        "cotangents": scatter_about(splits[7], (2 * N_FSDP * SLOTS, SEQ, D), 1.0, 6.0, ((0, 128),)),
        "rewards": jnp.clip(4.0 * jax.random.uniform(splits[8], (2 * N_FSDP * SLOTS,), jnp.float32) ** block_levels(splits[8], (2 * N_FSDP * SLOTS,), ((0, 128),), -0.2, 0.2), 0.0, 4.0),
        "prompt_keys": draw_prompt_keys(jax.random.fold_in(splits[15], 71), 0),
        "completion_lengths": place_ends(jax.random.randint(splits[10], (2 * N_FSDP * SLOTS,), 1, SEQ + 1), jax.random.fold_in(splits[10], 1), 1, SEQ).astype(jnp.int32),
        "finished_counts": draw_finished_counts(jax.random.fold_in(splits[15], 71), 0),
        "gate_weight": scatter_about(splits[12], (D, FF), D ** -0.5, 0.078125, ((1, 64),)),
        "up_weight": scatter_about(splits[13], (D, FF), D ** -0.5, 0.078125, ((1, 64),)),
        "down_weight": scatter_about(splits[14], (FF, D), FF ** -0.5, 0.0390625, ((0, 64),)),
    }


def gelu_pair(values):
    inner_arg = 0.7978845608028654 * (values + 0.044715 * values * values * values)
    tangent = jnp.tanh(inner_arg)
    result = 0.5 * values * (1.0 + tangent)
    slope_value = 0.5 * (1.0 + tangent) + 0.5 * values * (1.0 - tangent * tangent) * 0.7978845608028654 * (1.0 + 3.0 * 0.044715 * values * values)
    return (result, slope_value)

def attend_sample(inputs):
    query_block, fresh_keys, fresh_values, old_keys, old_values, length = inputs
    grouped = HEADS // KV_HEADS
    query_block = query_block.astype(jnp.float32).reshape(2, KV_HEADS, grouped, HEAD_DIM)
    fresh_keys = fresh_keys.astype(jnp.float32).reshape(2, KV_HEADS, HEAD_DIM)
    fresh_values = fresh_values.astype(jnp.float32).reshape(2, KV_HEADS, HEAD_DIM)
    old_keys = old_keys.astype(jnp.float32).reshape(CL, KV_HEADS, HEAD_DIM)
    old_values = old_values.astype(jnp.float32).reshape(CL, KV_HEADS, HEAD_DIM)
    score_scale = float(QSCALAR) ** (-0.5)
    cache_scores = jnp.einsum('tkgd,pkd->tkgp', query_block, old_keys) * score_scale
    fresh_scores = jnp.einsum('tkgd,skd->tkgs', query_block, fresh_keys) * score_scale
    cache_mask = jnp.arange(CL) < length
    step_mask = jnp.arange(2)[None, :] <= jnp.arange(2)[:, None]
    cache_scores = jnp.where(cache_mask[None, None, None, :], cache_scores, -1e+30)
    fresh_scores = jnp.where(step_mask[:, None, None, :], fresh_scores, -1e+30)
    scores = jnp.concatenate([cache_scores, fresh_scores], axis=-1)
    row_max = lax.optimization_barrier(jnp.max(scores, axis=-1, keepdims=True))
    weights = jnp.exp(scores - row_max)
    probabilities = (weights / lax.optimization_barrier(jnp.sum(weights, axis=-1, keepdims=True))).astype(jnp.bfloat16)
    all_values = jnp.concatenate([old_values, fresh_values], axis=0)
    combined = jnp.einsum('tkgp,pkd->tkgd', probabilities.astype(jnp.float32), all_values)
    return combined.reshape(2, HEADS * HEAD_DIM).astype(jnp.bfloat16)

def reference(queries, new_keys, new_values, cache_keys, cache_values, context_lengths, rollout_rows, cotangents, rewards, prompt_keys, completion_lengths, finished_counts, gate_weight, up_weight, down_weight):
    attended = lax.map(attend_sample, (queries, new_keys, new_values, cache_keys, cache_values, context_lengths))
    slot_total = rewards.shape[0]
    device_of = (jnp.arange(slot_total) // SLOTS).astype(jnp.int32)
    live_slot = jnp.arange(slot_total) % SLOTS < finished_counts[device_of]
    member = ((prompt_keys[:, None] == jnp.arange(GROUPS)[None, :]) & live_slot[:, None]).astype(jnp.float32)
    group_sum = lax.optimization_barrier(jnp.sum(member * rewards[:, None], axis=0))
    group_sq = lax.optimization_barrier(jnp.sum(member * (rewards * rewards)[:, None], axis=0))
    group_mean = group_sum / GROUP
    spread = group_sq / GROUP - group_mean * group_mean
    denominator = jnp.maximum(jnp.sqrt(jnp.maximum(spread, 0.0)), 1.0)
    slot_mean = lax.optimization_barrier(jnp.sum(member * group_mean[None, :], axis=1))
    slot_scale = lax.optimization_barrier(jnp.sum(member * denominator[None, :], axis=1))
    advantage = jnp.where(live_slot, (rewards - slot_mean) / jnp.where(live_slot, slot_scale, 1.0), 0.0)
    lengths_float = completion_lengths.astype(jnp.float32)
    token_live = jnp.arange(SEQ)[None, :] < completion_lengths[:, None]
    token_weight = jnp.where(token_live, advantage[:, None] / lengths_float[:, None], 0.0)
    scaled = (cotangents.astype(jnp.float32) * token_weight[:, :, None]).astype(jnp.bfloat16)
    row_block = rollout_rows.reshape(-1, D)
    scaled_block = scaled.reshape(-1, D)
    gate_value = jnp.dot(row_block, gate_weight, preferred_element_type=jnp.float32)
    up_value = jnp.dot(row_block, up_weight, preferred_element_type=jnp.float32)
    active, slope_value = gelu_pair(gate_value)
    hidden = (active * up_value).astype(jnp.bfloat16)
    back_grad = jnp.dot(scaled_block, down_weight.T, preferred_element_type=jnp.float32)
    d_gate = (back_grad * up_value * slope_value).astype(jnp.bfloat16)
    d_up = (back_grad * active).astype(jnp.bfloat16)
    grad_gate = jnp.dot(row_block.T, d_gate, preferred_element_type=jnp.float32).astype(jnp.bfloat16)
    grad_up = jnp.dot(row_block.T, d_up, preferred_element_type=jnp.float32).astype(jnp.bfloat16)
    grad_down = jnp.dot(hidden.T, scaled_block, preferred_element_type=jnp.float32).astype(jnp.bfloat16)
    return (attended, grad_gate, grad_up, grad_down)
```

```python
import functools

import jax
import jax.numpy as jnp
from jax import lax
from jax.experimental import pallas as pl
from jax.experimental.pallas import tpu as pltpu
from jax.sharding import PartitionSpec as P

HEADS = 32
KV_HEADS = 16
HEAD_DIM = 128
QSCALAR = 168
GROUP = 16
GROUPS = 8
CL = 256
D = 5376
HALF = 2688
HID = 336
TOK = 16
MESH = pl.DeviceIdType.MESH
NT = (((1,), (1,)), ((), ()))


def gelu_pair(values):
    inner_arg = 0.7978845608028654 * (values + 0.044715 * values * values * values)
    tangent = jnp.tanh(inner_arg)
    result = 0.5 * values * (1.0 + tangent)
    slope_value = 0.5 * (1.0 + tangent) + 0.5 * values * (
        1.0 - tangent * tangent
    ) * 0.7978845608028654 * (1.0 + 3.0 * 0.044715 * values * values)
    return (result, slope_value)


def attend_kernel(length, query, fresh_key, fresh_value, keys, values, out, scores, probs, mixed):
    scale = float(QSCALAR) ** (-0.5)
    valid = length[pl.program_id(0)]

    def stack(ref, count):
        wide = ref[0].astype(jnp.float32)
        parts = [wide[:, j * HEAD_DIM : (j + 1) * HEAD_DIM] for j in range(count)]
        return jnp.concatenate(parts, axis=0)

    asked = stack(query, HEADS)
    new_keys = stack(fresh_key, KV_HEADS).astype(jnp.bfloat16)
    new_values = stack(fresh_value, KV_HEADS).astype(jnp.bfloat16)
    for k in range(KV_HEADS):
        scores[4 * k : 4 * k + 4, :] = lax.dot_general(
            asked[4 * k : 4 * k + 4].astype(jnp.bfloat16),
            keys[0, :, k * HEAD_DIM : (k + 1) * HEAD_DIM],
            NT,
            preferred_element_type=jnp.float32,
        )
    fresh = lax.dot_general(
        asked.astype(jnp.bfloat16), new_keys, NT, preferred_element_type=jnp.float32
    )
    row = lax.broadcasted_iota(jnp.int32, (64, 32), 0)
    column = lax.broadcasted_iota(jnp.int32, (64, 32), 1)
    seen = (lax.div(row, 4) == lax.div(column, 2)) & (lax.rem(column, 2) <= lax.rem(row, 2))
    fresh = jnp.where(seen, fresh * scale, -1e30)
    position = lax.broadcasted_iota(jnp.int32, (64, CL), 1)
    cached = jnp.where(position < valid, scores[...] * scale, -1e30)
    top = jnp.maximum(
        jnp.max(cached, axis=-1, keepdims=True), jnp.max(fresh, axis=-1, keepdims=True)
    )
    cached = jnp.exp(cached - top)
    fresh = jnp.exp(fresh - top)
    total = jnp.sum(cached, axis=-1, keepdims=True) + jnp.sum(fresh, axis=-1, keepdims=True)
    probs[...] = cached / total
    fresh = (fresh / total).astype(jnp.bfloat16)
    mixed[...] = jnp.dot(fresh, new_values, preferred_element_type=jnp.float32)
    for k in range(KV_HEADS):
        mixed[4 * k : 4 * k + 4, :] += jnp.dot(
            probs[4 * k : 4 * k + 4, :].astype(jnp.bfloat16),
            values[0, :, k * HEAD_DIM : (k + 1) * HEAD_DIM],
            preferred_element_type=jnp.float32,
        )
    done = mixed[...]
    out[0] = jnp.concatenate(
        [done[2 * j : 2 * j + 2] for j in range(HEADS)], axis=1
    ).astype(jnp.bfloat16)


def attend(queries, new_keys, new_values, cache_keys, cache_values, context_lengths):
    samples = queries.shape[0]

    def block(*shape):
        return pl.BlockSpec((1,) + shape, lambda s: (s, 0, 0))

    return pl.pallas_call(
        attend_kernel,
        grid=(samples,),
        out_shape=jax.ShapeDtypeStruct(queries.shape, jnp.bfloat16),
        in_specs=[
            pl.BlockSpec(memory_space=pltpu.SMEM),
            block(2, 4096),
            block(2, 2048),
            block(2, 2048),
            block(CL, 2048),
            block(CL, 2048),
        ],
        out_specs=block(2, 4096),
        scratch_shapes=[
            pltpu.VMEM((64, CL), jnp.float32),
            pltpu.VMEM((64, CL), jnp.float32),
            pltpu.VMEM((64, HEAD_DIM), jnp.float32),
        ],
        compiler_params=pltpu.CompilerParams(vmem_limit_bytes=24 * 1024 * 1024),
    )(context_lengths, queries, new_keys, new_values, cache_keys, cache_values)


def place():
    role = lax.axis_index("role")
    index = lax.axis_index("fsdp")
    return (
        role,
        lax.div(index, 32),
        lax.rem(lax.div(index, 8), 4),
        lax.rem(lax.div(index, 2), 4),
        lax.rem(index, 2),
    )


def device(role, high, x, y, core):
    return {"role": role, "fsdp": ((high * 4 + x) * 4 + y) * 2 + core}


def flip(bit, other):
    return lax.rem(bit + other, 2)


def turn(pos, step):
    return lax.rem(pos + step, 4)


def meet(partners):
    barrier = pltpu.get_barrier_semaphore()
    for partner in partners:
        pl.semaphore_signal(barrier, inc=1, device_id=partner, device_id_type=MESH)
    pl.semaphore_wait(barrier, len(partners))


def remote(src, dst, send, recv, target):
    return pltpu.make_async_remote_copy(
        src_ref=src,
        dst_ref=dst,
        send_sem=send,
        recv_sem=recv,
        device_id=target,
        device_id_type=MESH,
    )


def pack_kernel(
    count, reward, key, length, rows, cots,
    out_rows, out_cots, info,
    src, got, meta, token, col_send, ring_send, data_recv,
    mcol_recv, mx_send, mx_recv, my_send, my_recv,
):
    role, high, x, y, core = place()
    mine = high * 2 + core
    pos = (x, y)
    offsets = [(dr, dh, dc) for dr in (0, 1) for dh in (0, 1) for dc in (0, 1)][1:]
    column = [
        device(flip(role, dr), flip(high, dh), x, y, flip(core, dc)) for dr, dh, dc in offsets
    ]
    x_line = [device(role, high, turn(x, s), y, core) for s in (1, 2, 3)]
    y_line = [device(role, high, x, turn(y, s), core) for s in (1, 2, 3)]
    line = (x_line, y_line)
    neighbour = ((x_line[0], x_line[2]), (y_line[0], y_line[2]))
    meet(column + x_line + y_line)

    copies = []

    def send(src_ref, dst_ref, send_sem, recv_sem, target):
        copy = remote(src_ref, dst_ref, send_sem, recv_sem, target)
        copy.start()
        return copy

    def arrived(ref, sem):
        remote(ref, ref, sem, sem, x_line[0]).wait_recv()

    def column_copies():
        made = []
        for i, (dr, dh, dc) in enumerate(offsets):
            made.append(
                remote(
                    meta.at[y, x, mine], meta.at[y, x, mine],
                    col_send.at[i, 2], mcol_recv.at[mine], column[i],
                )
            )
        for i, (dr, dh, dc) in enumerate(offsets):
            part = flip(core, dc)
            for a in (0, 1):
                made.append(
                    remote(
                        src.at[a, part], got.at[a, pos[a], mine],
                        col_send.at[i, a], data_recv.at[a, pos[a], mine], column[i],
                    )
                )
        return made

    lane = lax.broadcasted_iota(jnp.int32, (8, 128), 1)
    sub = lax.broadcasted_iota(jnp.int32, (8, 128), 0)

    @pl.when(role == 0)
    def _():
        base = (lax.rem(x, 2) * 4 + mine) * TOK
        tile = jnp.zeros((8, 128), jnp.float32)
        for s in range(4):
            here = (lane >= base + 4 * s) & (lane < base + 4 * s + 4)
            live = jnp.where(s < count[0], 1.0, 0.0)
            value = jnp.where(
                sub == 0,
                reward[s],
                jnp.where(
                    sub == 1,
                    key[s].astype(jnp.float32),
                    jnp.where(
                        sub == 2,
                        length[s].astype(jnp.float32),
                        jnp.where(sub == 3, live, 0.0),
                    ),
                ),
            )
            tile = jnp.where(here, value, tile)
        meta[y, x, mine] = tile
        for a, ref in enumerate((rows, cots)):
            wide = jnp.concatenate(
                [ref[s].astype(jnp.float32) for s in range(4)], axis=0
            ).astype(jnp.bfloat16)
            src[a, 0] = wide[:, :HALF]
            src[a, 1] = wide[:, HALF:]
        for copy in column_copies():
            copy.start()
        for a in (0, 1):
            got[a, pos[a], mine] = src[a, core]

    blocks = [
        flip(high, dh) * 2 + flip(core, dc) for dh, dc in ((0, 0), (0, 1), (1, 0), (1, 1))
    ]

    def wait_column(k, what):
        if k == 0:
            @pl.when(role == 1)
            def _():
                what()
        else:
            what()

    for k, block in enumerate(blocks):
        wait_column(
            k, lambda block=block: arrived(meta.at[y, x, block], mcol_recv.at[block])
        )
    for i in range(3):
        copies.append(
            send(meta.at[y, x], meta.at[y, x], mx_send.at[i], mx_recv.at[x], x_line[i])
        )
    for k, block in enumerate(blocks):
        for a in (0, 1):
            here = got.at[a, pos[a], block]
            wait_column(
                k,
                lambda here=here, a=a, block=block: arrived(
                    here, data_recv.at[a, pos[a], block]
                ),
            )
            for way in (0, 1):
                copies.append(
                    send(
                        here, here, ring_send.at[a, way, k],
                        data_recv.at[a, pos[a], block], neighbour[a][way],
                    )
                )
    for i in (1, 2, 3):
        other = turn(x, i)
        arrived(meta.at[y, other], mx_recv.at[other])
    for i in range(3):
        copies.append(send(meta.at[y], meta.at[y], my_send.at[i], my_recv.at[y], y_line[i]))
    for i in (0, 1):
        for a in (0, 1):
            for way in (0, 1):
                origin = turn(pos[a], 3 if way == 0 else 1)
                block = 2 * i + way
                here = got.at[a, origin, block]
                arrived(here, data_recv.at[a, origin, block])
                copies.append(
                    send(
                        here, here, ring_send.at[a, way, 4 + i],
                        data_recv.at[a, origin, block], neighbour[a][way],
                    )
                )
    for i in (1, 2, 3):
        other = turn(y, i)
        arrived(meta.at[other], my_recv.at[other])

    tiles = []
    for s in range(8):
        total = jnp.zeros((8, 128), jnp.float32)
        for xi in (0, 1):
            for block in range(4):
                total = total + meta[s // 2, (s % 2) * 2 + xi, block]
        tiles.append(total)
    rewards, keys, lengths, live = (
        jnp.concatenate([t[q : q + 1] for t in tiles], axis=0) for q in range(4)
    )
    step = lax.rem(lane, 4).astype(jnp.float32)
    first = jnp.where(step == 0.0, live, 0.0)
    mean = jnp.zeros((8, 128), jnp.float32)
    denominator = jnp.ones((8, 128), jnp.float32)
    for k in range(GROUPS):
        same = keys == float(k)
        member = jnp.where(same, first, 0.0)
        group_sum = jnp.sum(member * rewards, axis=(0, 1), keepdims=True)
        group_sq = jnp.sum(member * (rewards * rewards), axis=(0, 1), keepdims=True)
        group_mean = group_sum / GROUP
        spread = group_sq / GROUP - group_mean * group_mean
        divisor = jnp.maximum(jnp.sqrt(jnp.maximum(spread, 0.0)), 1.0)
        mean = jnp.where(same, group_mean, mean)
        denominator = jnp.where(same, divisor, denominator)
    used = (live > 0.0) & (step < lengths)
    mask = jnp.where(used, 1.0, 0.0)
    weight = jnp.where(used, (rewards - mean) / denominator / jnp.maximum(lengths, 1.0), 0.0)

    a_lane = lax.broadcasted_iota(jnp.int32, (128, 128), 0)
    b_lane = lax.broadcasted_iota(jnp.int32, (128, 128), 1)
    same_column = (a_lane < 64) == (b_lane < 64)

    def count_by(take):
        return jnp.dot(
            mask.astype(jnp.bfloat16),
            jnp.where(take, 1.0, 0.0).astype(jnp.bfloat16),
            preferred_element_type=jnp.float32,
        )

    before_all = count_by(a_lane < b_lane)
    before_column = count_by((a_lane < b_lane) & same_column)
    whole = jnp.sum(mask, axis=1, keepdims=True) + jnp.zeros((8, 128), jnp.float32)
    own_column = count_by(same_column)
    rank_y_rows, rank_x_rows = [], []
    for s in range(8):
        ry = before_all[s : s + 1]
        if s % 2 == 1:
            ry = ry + whole[s - 1 : s]
        rx = before_column[s : s + 1]
        for t in range(s % 2, s, 2):
            rx = rx + own_column[t : t + 1]
        rank_y_rows.append(ry)
        rank_x_rows.append(rx)
    rank_y = jnp.concatenate(rank_y_rows, axis=0)
    rank_x = jnp.concatenate(rank_x_rows, axis=0)
    load = jnp.zeros((1, 1), jnp.float32)
    for g in range(4):
        in_y = jnp.where(lax.div(sub, 2) == g, mask, 0.0)
        in_x = jnp.where(lax.rem(sub, 2) * 2 + lax.div(lane, 64) == g, mask, 0.0)
        load = jnp.maximum(load, jnp.sum(in_y, axis=(0, 1), keepdims=True))
        load = jnp.maximum(load, jnp.sum(in_x, axis=(0, 1), keepdims=True))
    info[0] = jnp.where(used, rank_y, -1.0)
    info[1] = jnp.where(used, rank_x, -1.0)
    info[2] = mask
    info[3] = load + jnp.zeros((8, 128), jnp.float32)

    token[0] = jnp.where(used, rank_y, -1.0)
    swapped = lax.rem(x, 2) == 1
    for q, value in ((1, jnp.where(used, rank_x, -1.0)), (2, weight)):
        rolled = pltpu.roll(value, 64, 1)
        token[q] = jnp.where(swapped, rolled, value)
        token[q + 2] = jnp.where(swapped, value, rolled)

    def y_row(q):
        return jnp.concatenate(
            [token[q, pl.ds(2 * y, 1), :], token[q, pl.ds(2 * y + 1, 1), :]], axis=1
        )

    def x_row(q):
        low = lax.broadcasted_iota(jnp.int32, (1, 128), 1) < 64
        half_x = lax.div(x, 2)
        parts = [
            jnp.where(
                low,
                token[q, pl.ds(2 * t + half_x, 1), :],
                token[q + 2, pl.ds(2 * t + 2 + half_x, 1), :],
            )
            for t in (0, 2)
        ]
        return jnp.concatenate(parts, axis=1)

    target = lax.broadcasted_iota(jnp.int32, (256, 256), 0).astype(jnp.float32)
    pick_rows = jnp.where(target == y_row(0), 1.0, 0.0).astype(jnp.bfloat16)
    chosen = target == x_row(1)
    pick_cots = jnp.where(chosen, 1.0, 0.0).astype(jnp.bfloat16)
    row_weight = jnp.sum(jnp.where(chosen, x_row(2), 0.0), axis=1, keepdims=True)

    for a in (0, 1):
        for way in (0, 1):
            origin = turn(pos[a], 3 if way == 0 else 1)
            for block in range(4):
                if block % 2 != way:
                    arrived(got.at[a, origin, block], data_recv.at[a, origin, block])
        origin = turn(pos[a], 2)
        for block in range(4):
            arrived(got.at[a, origin, block], data_recv.at[a, origin, block])

    for part in range(7):
        cols = slice(part * 384, (part + 1) * 384)
        block = got[0, :, :, :, cols].reshape(256, 384)
        out_rows[:, cols] = jnp.dot(
            pick_rows, block, preferred_element_type=jnp.float32
        ).astype(jnp.bfloat16)
        block = got[1, :, :, :, cols].reshape(256, 384)
        packed = jnp.dot(pick_cots, block, preferred_element_type=jnp.float32)
        out_cots[:, cols] = (packed * row_weight).astype(jnp.bfloat16)

    for copy in copies:
        copy.wait_send()

    @pl.when(role == 0)
    def _():
        for copy in column_copies():
            copy.wait_send()


def pack(count, rewards, keys, lengths, rows, cots):
    smem = pl.BlockSpec(memory_space=pltpu.SMEM)
    vmem = pl.BlockSpec(memory_space=pltpu.VMEM)
    return pl.pallas_call(
        pack_kernel,
        out_shape=(
            jax.ShapeDtypeStruct((256, HALF), jnp.bfloat16),
            jax.ShapeDtypeStruct((256, HALF), jnp.bfloat16),
            jax.ShapeDtypeStruct((4, 8, 128), jnp.float32),
        ),
        in_specs=[smem] * 4 + [vmem] * 2,
        out_specs=(vmem, vmem, vmem),
        scratch_shapes=[
            pltpu.VMEM((2, 2, TOK, HALF), jnp.bfloat16),
            pltpu.VMEM((2, 4, 4, TOK, HALF), jnp.bfloat16),
            pltpu.VMEM((4, 4, 4, 8, 128), jnp.float32),
            pltpu.VMEM((5, 8, 128), jnp.float32),
            pltpu.SemaphoreType.DMA((7, 3)),
            pltpu.SemaphoreType.DMA((2, 2, 6)),
            pltpu.SemaphoreType.DMA((2, 4, 4)),
            pltpu.SemaphoreType.DMA((4,)),
            pltpu.SemaphoreType.DMA((3,)),
            pltpu.SemaphoreType.DMA((4,)),
            pltpu.SemaphoreType.DMA((3,)),
            pltpu.SemaphoreType.DMA((4,)),
        ],
        compiler_params=pltpu.CompilerParams(
            collective_id=1, has_side_effects=True, vmem_limit_bytes=32 * 1024 * 1024
        ),
    )(count, rewards, keys, lengths, rows, cots)


def forward_kernel(
    cap, packed_rows, packed_cots, info, w_gate, w_up, w_down,
    d_gate, d_up, hidden, out_rows, out_cots,
    held, weights, acc, row_hot, cot_hot, perm,
    own_send, relay_send, pass_send, recv, local_sem,
):
    role, high, x, y, core = place()
    pos = (y, x)
    parts = 4
    rows = cap // parts
    sibling = device(role, high, x, y, flip(core, 1))
    neighbour = (
        (device(role, high, x, turn(y, 1), core), device(role, high, x, turn(y, 3), core)),
        (device(role, high, turn(x, 1), y, core), device(role, high, turn(x, 3), y, core)),
    )
    source = (packed_rows, packed_cots)
    local = [
        pltpu.make_async_copy(source[a].at[pl.ds(0, cap)], held.at[a, core, pos[a]], local_sem.at[a])
        for a in (0, 1)
    ] + [
        pltpu.make_async_copy(w, weights.at[i], local_sem.at[2 + i])
        for i, w in enumerate((w_gate, w_up, w_down))
    ]
    for copy in local:
        copy.start()
    meet([sibling, *neighbour[0], *neighbour[1]])

    copies = []

    def send(src, a, half, group, part, send_sem, target):
        dst = held.at[a, half, group, pl.ds(part * rows, rows)]
        copy = remote(
            dst if src is None else src, dst, send_sem, recv.at[a, half, group, part], target
        )
        copy.start()
        copies.append(copy)

    def arrived(a, half, group, part):
        ref = held.at[a, half, group, pl.ds(part * rows, rows)]
        remote(ref, ref, recv.at[a, half, group, part], recv.at[a, half, group, part], sibling).wait_recv()

    for i in range(parts):
        for a in (0, 1):
            for way, part in ((0, i), (1, (i + 2) % 4), (2, i)):
                target = sibling if way == 2 else neighbour[a][way]
                src = source[a].at[pl.ds(part * rows, rows)]
                send(src, a, core, pos[a], part, own_send.at[a, way, part], target)

    other = flip(core, 1)

    def product(which, a, group):
        cols = pl.ds(pl.multiple_of(group * cap, 128), cap)
        total = None
        for half in (0, 1):
            term = lax.dot_general(
                weights[which, :, half * HALF : (half + 1) * HALF],
                held[a, half, group],
                NT,
                preferred_element_type=jnp.float32,
            )
            total = term if total is None else total + term
        acc[which, :, cols] = total

    def products(step):
        for which, a in ((0, 0), (1, 0), (2, 1)):
            product(which, a, turn(pos[a], step))

    lane = lax.broadcasted_iota(jnp.int32, (1, 128), 1)
    place_at = lax.broadcasted_iota(jnp.int32, (4 * cap, 128), 0).astype(jnp.float32)
    for s in range(8):
        cols = slice(s * 128, (s + 1) * 128)
        used = info[2, s : s + 1, :] > 0.0
        in_rows = info[0, s : s + 1, :] + float((s // 2) * cap)
        x_of = (lax.div(lane, 64) + (s % 2) * 2).astype(jnp.float32)
        in_cots = info[1, s : s + 1, :] + x_of * float(cap)
        in_rows = jnp.where(used, in_rows, -1.0)
        in_cots = jnp.where(used, in_cots, -1.0)
        row_hot[:, cols] = jnp.where(place_at == in_rows, 1.0, 0.0).astype(jnp.bfloat16)
        cot_hot[:, cols] = jnp.where(place_at == in_cots, 1.0, 0.0).astype(jnp.bfloat16)

    @pl.loop(0, 4 * cap // 128)
    def _(i):
        some = pl.ds(pl.multiple_of(i * 128, 128), 128)
        perm[some, :] = lax.dot_general(
            cot_hot[some, :], row_hot[...], NT, preferred_element_type=jnp.float32
        ).astype(jnp.bfloat16)

    for copy in local:
        copy.wait()
    for a in (0, 1):
        for part in range(parts):
            arrived(a, other, pos[a], part)
    products(0)

    for i in range(parts):
        for a in (0, 1):
            for way, part in ((0, i), (1, (i + 2) % 4)):
                group = turn(pos[a], 3 if way == 0 else 1)
                arrived(a, core, group, part)
                if i < 2:
                    send(None, a, core, group, part, relay_send.at[a, part], neighbour[a][way])
                send(None, a, core, group, part, pass_send.at[a, way, part], sibling)
    for step in (1, 3):
        for a in (0, 1):
            for part in range(parts):
                arrived(a, other, turn(pos[a], step), part)
        products(step)
    for part in (0, 2, 1, 3):
        for a in (0, 1):
            group = turn(pos[a], 2)
            arrived(a, core, group, part)
            send(None, a, core, group, part, pass_send.at[a, 2, part], sibling)
    for part in (0, 2, 1, 3):
        for a in (0, 1):
            arrived(a, other, turn(pos[a], 2), part)
    result = [
        pltpu.make_async_copy(held.at[a, role], out, local_sem.at[a])
        for a, out in ((0, out_rows), (1, out_cots))
    ]
    for copy in result:
        copy.start()
    products(2)

    for i in range(4 * cap // 128):
        cols = slice(i * 128, (i + 1) * 128)
        back = acc[2]
        upper = back.astype(jnp.bfloat16)
        lower = (back - upper.astype(jnp.float32)).astype(jnp.bfloat16)
        back = jnp.dot(upper, perm[:, cols], preferred_element_type=jnp.float32) + jnp.dot(
            lower, perm[:, cols], preferred_element_type=jnp.float32
        )
        gate = acc[0, :, cols]
        up = acc[1, :, cols]
        active, slope = gelu_pair(gate)
        d_gate[:, cols] = (back * up * slope).astype(jnp.bfloat16)
        d_up[:, cols] = (back * active).astype(jnp.bfloat16)
        row_hot[0:HID, cols] = (active * up).astype(jnp.bfloat16)
    for i in range(4 * cap // 128):
        cols = slice(i * 128, (i + 1) * 128)
        hidden[:, cols] = lax.dot_general(
            row_hot[0:HID, 0 : 4 * cap], perm[cols, :], NT, preferred_element_type=jnp.float32
        ).astype(jnp.bfloat16)

    for copy in copies:
        copy.wait_send()
    for copy in result:
        copy.wait()


def forward(cap, packed_rows, packed_cots, info, w_gate, w_up, w_down):
    vmem = pl.BlockSpec(memory_space=pltpu.VMEM)
    hbm = pl.BlockSpec(memory_space=pl.ANY)
    small = jax.ShapeDtypeStruct((HID, 4 * cap), jnp.bfloat16)
    large = jax.ShapeDtypeStruct((4, cap, HALF), jnp.bfloat16)
    d_gate, d_up, hidden, rows, cots = pl.pallas_call(
        functools.partial(forward_kernel, cap),
        out_shape=(small, small, small, large, large),
        in_specs=[hbm, hbm, vmem, hbm, hbm, hbm],
        out_specs=(vmem, vmem, vmem, hbm, hbm),
        scratch_shapes=[
            pltpu.VMEM((2, 2, 4, cap, HALF), jnp.bfloat16),
            pltpu.VMEM((3, HID, D), jnp.bfloat16),
            pltpu.VMEM((3, HID, 4 * cap), jnp.float32),
            pltpu.VMEM((4 * cap, 1024), jnp.bfloat16),
            pltpu.VMEM((4 * cap, 1024), jnp.bfloat16),
            pltpu.VMEM((4 * cap, 4 * cap), jnp.bfloat16),
            pltpu.SemaphoreType.DMA((2, 3, 4)),
            pltpu.SemaphoreType.DMA((2, 4)),
            pltpu.SemaphoreType.DMA((2, 3, 4)),
            pltpu.SemaphoreType.DMA((2, 2, 4, 4)),
            pltpu.SemaphoreType.DMA((5,)),
        ],
        compiler_params=pltpu.CompilerParams(
            collective_id=2 if cap == 128 else 3,
            has_side_effects=True,
            vmem_limit_bytes=60 * 1024 * 1024,
        ),
    )(packed_rows, packed_cots, info, w_gate, w_up, w_down)
    rows = rows.reshape(4 * cap, HALF)
    cots = cots.reshape(4 * cap, HALF)
    return tuple(
        jnp.dot(left, right, preferred_element_type=jnp.float32).astype(jnp.bfloat16)
        for left, right in ((d_gate, rows), (d_up, rows), (hidden, cots))
    )


def local(
    queries, new_keys, new_values, cache_keys, cache_values, context_lengths,
    rollout_rows, cotangents, rewards, prompt_keys, completion_lengths, finished_counts,
    gate_weight, up_weight, down_weight,
):
    attended = attend(queries, new_keys, new_values, cache_keys, cache_values, context_lengths)
    packed_rows, packed_cots, info = pack(
        finished_counts, rewards, prompt_keys, completion_lengths, rollout_rows, cotangents
    )
    operands = (packed_rows, packed_cots, info, gate_weight.T, up_weight.T, down_weight)
    grad_gate, grad_up, grad_down = lax.cond(
        info[3, 0, 0] <= 128.0,
        functools.partial(forward, 128),
        functools.partial(forward, 256),
        *operands,
    )
    return (attended, grad_gate.T, grad_up.T, grad_down)


def solution(mesh):
    return jax.shard_map(
        local,
        mesh=mesh,
        in_specs=(
            P("fsdp", None, None),
            P("fsdp", None, None),
            P("fsdp", None, None),
            P("fsdp", None, None),
            P("fsdp", None, None),
            P("fsdp"),
            P(("role", "fsdp"), None, None),
            P(("role", "fsdp"), None, None),
            P(("role", "fsdp")),
            P(("role", "fsdp")),
            P(("role", "fsdp")),
            P(("role", "fsdp")),
            P(None, "fsdp"),
            P(None, "fsdp"),
            P("fsdp", None),
        ),
        out_specs=(P("fsdp", None, None), P("role", "fsdp"), P("role", "fsdp"), P("fsdp", "role")),
        check_vma=False,
    )
```

```python
import functools

import jax
import jax.numpy as jnp
from jax import lax
from jax.experimental import pallas as pl
from jax.experimental.pallas import tpu as pltpu
from jax.sharding import PartitionSpec as P

HEADS = 32
KV_HEADS = 16
HEAD_DIM = 128
QSCALAR = 168
GROUP = 16
GROUPS = 8
CL = 256
D = 5376
HALF = 2688
HID = 336
TOK = 16
MESH = pl.DeviceIdType.MESH
NT = (((1,), (1,)), ((), ()))


def gelu_pair(values):
    inner_arg = 0.7978845608028654 * (values + 0.044715 * values * values * values)
    tangent = jnp.tanh(inner_arg)
    result = 0.5 * values * (1.0 + tangent)
    slope_value = 0.5 * (1.0 + tangent) + 0.5 * values * (
        1.0 - tangent * tangent
    ) * 0.7978845608028654 * (1.0 + 3.0 * 0.044715 * values * values)
    return (result, slope_value)


def attend_sample(s, valid, query, fresh_key, fresh_value, keys, values, out, scores, probs, mixed):
    scale = float(QSCALAR) ** (-0.5)

    def stack(ref, count):
        wide = ref[s].astype(jnp.float32)
        parts = [wide[:, j * HEAD_DIM : (j + 1) * HEAD_DIM] for j in range(count)]
        return jnp.concatenate(parts, axis=0)

    asked = stack(query, HEADS)
    new_keys = stack(fresh_key, KV_HEADS).astype(jnp.bfloat16)
    new_values = stack(fresh_value, KV_HEADS).astype(jnp.bfloat16)
    for k in range(KV_HEADS):
        scores[4 * k : 4 * k + 4, :] = lax.dot_general(
            asked[4 * k : 4 * k + 4].astype(jnp.bfloat16),
            keys[s, :, k * HEAD_DIM : (k + 1) * HEAD_DIM],
            NT,
            preferred_element_type=jnp.float32,
        )
    fresh = lax.dot_general(
        asked.astype(jnp.bfloat16), new_keys, NT, preferred_element_type=jnp.float32
    )
    row = lax.broadcasted_iota(jnp.int32, (64, 32), 0)
    column = lax.broadcasted_iota(jnp.int32, (64, 32), 1)
    seen = (lax.div(row, 4) == lax.div(column, 2)) & (lax.rem(column, 2) <= lax.rem(row, 2))
    fresh = jnp.where(seen, fresh * scale, -1e30)
    position = lax.broadcasted_iota(jnp.int32, (64, CL), 1)
    cached = jnp.where(position < valid, scores[...] * scale, -1e30)
    top = jnp.maximum(
        jnp.max(cached, axis=-1, keepdims=True), jnp.max(fresh, axis=-1, keepdims=True)
    )
    cached = jnp.exp(cached - top)
    fresh = jnp.exp(fresh - top)
    total = jnp.sum(cached, axis=-1, keepdims=True) + jnp.sum(fresh, axis=-1, keepdims=True)
    probs[...] = cached / total
    fresh = (fresh / total).astype(jnp.bfloat16)
    mixed[...] = jnp.dot(fresh, new_values, preferred_element_type=jnp.float32)
    for k in range(KV_HEADS):
        mixed[4 * k : 4 * k + 4, :] += jnp.dot(
            probs[4 * k : 4 * k + 4, :].astype(jnp.bfloat16),
            values[s, :, k * HEAD_DIM : (k + 1) * HEAD_DIM],
            preferred_element_type=jnp.float32,
        )
    done = mixed[...]
    out[s] = jnp.concatenate(
        [done[2 * j : 2 * j + 2] for j in range(HEADS)], axis=1
    ).astype(jnp.bfloat16)


def place():
    role = lax.axis_index("role")
    index = lax.axis_index("fsdp")
    return (
        role,
        lax.div(index, 32),
        lax.rem(lax.div(index, 8), 4),
        lax.rem(lax.div(index, 2), 4),
        lax.rem(index, 2),
    )


def device(role, high, x, y, core):
    return {"role": role, "fsdp": ((high * 4 + x) * 4 + y) * 2 + core}


def flip(bit, other):
    return lax.rem(bit + other, 2)


def turn(pos, step):
    return lax.rem(pos + step, 4)


def meet(partners):
    barrier = pltpu.get_barrier_semaphore()
    for partner in partners:
        pl.semaphore_signal(barrier, inc=1, device_id=partner, device_id_type=MESH)
    pl.semaphore_wait(barrier, len(partners))


def remote(src, dst, send, recv, target):
    return pltpu.make_async_remote_copy(
        src_ref=src,
        dst_ref=dst,
        send_sem=send,
        recv_sem=recv,
        device_id=target,
        device_id_type=MESH,
    )


def pack_kernel(
    count_in, reward_in, key_in, length_in, context_in, rows_in, cots_in,
    query_in, fresh_key_in, fresh_value_in, keys_in, values_in,
    attended, out_rows, out_cots, info,
    count, reward, key, length, context, rows, cots, query, fresh_key, fresh_value,
    keys, values, scores, probs, mixed, load_sem, cache_sem,
    src, got, meta, token, col_send, ring_send, data_recv,
    mcol_recv, mx_send, mx_recv, my_send, my_recv,
):
    role, high, x, y, core = place()
    mine = high * 2 + core
    pos = (x, y)
    offsets = [(dr, dh, dc) for dr in (0, 1) for dh in (0, 1) for dc in (0, 1)][1:]
    column = [
        device(flip(role, dr), flip(high, dh), x, y, flip(core, dc)) for dr, dh, dc in offsets
    ]
    x_line = [device(role, high, turn(x, s), y, core) for s in (1, 2, 3)]
    y_line = [device(role, high, x, turn(y, s), core) for s in (1, 2, 3)]
    line = (x_line, y_line)
    neighbour = ((x_line[0], x_line[2]), (y_line[0], y_line[2]))
    loads = [
        pltpu.make_async_copy(a, b, load_sem.at[i])
        for i, (a, b) in enumerate(
            (
                (count_in, count), (reward_in, reward), (key_in, key), (length_in, length),
                (rows_in, rows), (cots_in, cots), (context_in, context), (query_in, query),
                (fresh_key_in, fresh_key), (fresh_value_in, fresh_value),
            )
        )
    ]
    caches = [
        [
            pltpu.make_async_copy(a.at[s], b.at[s], cache_sem.at[s, i])
            for i, (a, b) in enumerate(((keys_in, keys), (values_in, values)))
        ]
        for s in range(4)
    ]
    for copy in loads:
        copy.start()

    def attend(s):
        for copy in caches[s]:
            copy.wait()
        attend_sample(
            s, context[s], query, fresh_key, fresh_value, keys, values, attended,
            scores, probs, mixed,
        )

    for copy in loads[:6]:
        copy.wait()
    meet(column + x_line + y_line)

    copies = []

    def send(src_ref, dst_ref, send_sem, recv_sem, target):
        copy = remote(src_ref, dst_ref, send_sem, recv_sem, target)
        copy.start()
        return copy

    def arrived(ref, sem):
        remote(ref, ref, sem, sem, x_line[0]).wait_recv()

    def column_copies():
        made = []
        for i, (dr, dh, dc) in enumerate(offsets):
            made.append(
                remote(
                    meta.at[y, x, mine], meta.at[y, x, mine],
                    col_send.at[i, 2], mcol_recv.at[mine], column[i],
                )
            )
        for i, (dr, dh, dc) in enumerate(offsets):
            if dr == 0 and dh == 1:
                continue
            part = flip(core, dc)
            for a in (0, 1):
                made.append(
                    remote(
                        src.at[a, part], got.at[a, pos[a], mine],
                        col_send.at[i, a], data_recv.at[a, pos[a], mine], column[i],
                    )
                )
        return made

    lane = lax.broadcasted_iota(jnp.int32, (8, 128), 1)
    sub = lax.broadcasted_iota(jnp.int32, (8, 128), 0)

    @pl.when(role == 0)
    def _():
        base = (lax.rem(x, 2) * 4 + mine) * TOK
        tile = jnp.zeros((8, 128), jnp.float32)
        for s in range(4):
            here = (lane >= base + 4 * s) & (lane < base + 4 * s + 4)
            live = jnp.where(s < count[0], 1.0, 0.0)
            value = jnp.where(
                sub == 0,
                reward[s],
                jnp.where(
                    sub == 1,
                    key[s].astype(jnp.float32),
                    jnp.where(
                        sub == 2,
                        length[s].astype(jnp.float32),
                        jnp.where(sub == 3, live, 0.0),
                    ),
                ),
            )
            tile = jnp.where(here, value, tile)
        meta[y, x, mine] = tile
        for a, ref in enumerate((rows, cots)):
            wide = jnp.concatenate(
                [ref[s].astype(jnp.float32) for s in range(4)], axis=0
            ).astype(jnp.bfloat16)
            src[a, 0] = wide[:, :HALF]
            src[a, 1] = wide[:, HALF:]
        for copy in column_copies():
            copy.start()
        for a in (0, 1):
            got[a, pos[a], mine] = src[a, core]

    for pair in caches:
        for copy in pair:
            copy.start()
    for copy in loads[6:]:
        copy.wait()

    blocks = [
        flip(high, dh) * 2 + flip(core, dc) for dh, dc in ((0, 0), (0, 1), (1, 0), (1, 1))
    ]

    def handed_on(block, k):
        target = device(0, flip(lax.div(block, 2), 1), x, y, core)
        here = got.at[high, jnp.where(high == 0, x, y), block]
        return remote(
            here, here, col_send.at[k, 0], data_recv.at[high, jnp.where(high == 0, x, y), block], target
        )

    def wait_column(k, what):
        if k == 0:
            @pl.when(role == 1)
            def _():
                what()
        else:
            what()

    for k, block in enumerate(blocks):
        wait_column(
            k, lambda block=block: arrived(meta.at[y, x, block], mcol_recv.at[block])
        )
    for i in range(3):
        copies.append(
            send(meta.at[y, x], meta.at[y, x], mx_send.at[i], mx_recv.at[x], x_line[i])
        )
    for k, block in enumerate(blocks):
        @pl.when(role == 1)
        def _():
            arrived(
                got.at[high, jnp.where(high == 0, x, y), block],
                data_recv.at[high, jnp.where(high == 0, x, y), block],
            )
            handed_on(block, k).start()

        for a in (0, 1):
            here = got.at[a, pos[a], block]
            if k > 0:
                @pl.when(role == 0)
                def _():
                    arrived(here, data_recv.at[a, pos[a], block])

            @pl.when((role == 1) & (high != a))
            def _():
                arrived(here, data_recv.at[a, pos[a], block])

            for way in (0, 1):
                copies.append(
                    send(
                        here, here, ring_send.at[a, way, k],
                        data_recv.at[a, pos[a], block], neighbour[a][way],
                    )
                )
    attend(0)
    for i in (1, 2, 3):
        other = turn(x, i)
        arrived(meta.at[y, other], mx_recv.at[other])
    for i in range(3):
        copies.append(send(meta.at[y], meta.at[y], my_send.at[i], my_recv.at[y], y_line[i]))
    for i in (0, 1):
        for a in (0, 1):
            for way in (0, 1):
                origin = turn(pos[a], 3 if way == 0 else 1)
                block = 2 * i + way
                here = got.at[a, origin, block]
                arrived(here, data_recv.at[a, origin, block])
                copies.append(
                    send(
                        here, here, ring_send.at[a, way, 4 + i],
                        data_recv.at[a, origin, block], neighbour[a][way],
                    )
                )
    for i in (1, 2, 3):
        other = turn(y, i)
        arrived(meta.at[other], my_recv.at[other])

    attend(1)
    attend(2)
    attend(3)

    tiles = []
    for s in range(8):
        total = jnp.zeros((8, 128), jnp.float32)
        for xi in (0, 1):
            for block in range(4):
                total = total + meta[s // 2, (s % 2) * 2 + xi, block]
        tiles.append(total)
    rewards, keys, lengths, live = (
        jnp.concatenate([t[q : q + 1] for t in tiles], axis=0) for q in range(4)
    )
    step = lax.rem(lane, 4).astype(jnp.float32)
    first = jnp.where(step == 0.0, live, 0.0)
    mean = jnp.zeros((8, 128), jnp.float32)
    denominator = jnp.ones((8, 128), jnp.float32)
    for k in range(GROUPS):
        same = keys == float(k)
        member = jnp.where(same, first, 0.0)
        group_sum = jnp.sum(member * rewards, axis=(0, 1), keepdims=True)
        group_sq = jnp.sum(member * (rewards * rewards), axis=(0, 1), keepdims=True)
        group_mean = group_sum / GROUP
        spread = group_sq / GROUP - group_mean * group_mean
        divisor = jnp.maximum(jnp.sqrt(jnp.maximum(spread, 0.0)), 1.0)
        mean = jnp.where(same, group_mean, mean)
        denominator = jnp.where(same, divisor, denominator)
    used = (live > 0.0) & (step < lengths)
    mask = jnp.where(used, 1.0, 0.0)
    weight = jnp.where(used, (rewards - mean) / denominator / jnp.maximum(lengths, 1.0), 0.0)

    a_lane = lax.broadcasted_iota(jnp.int32, (128, 128), 0)
    b_lane = lax.broadcasted_iota(jnp.int32, (128, 128), 1)
    same_column = (a_lane < 64) == (b_lane < 64)

    def count_by(take):
        return jnp.dot(
            mask.astype(jnp.bfloat16),
            jnp.where(take, 1.0, 0.0).astype(jnp.bfloat16),
            preferred_element_type=jnp.float32,
        )

    before_all = count_by(a_lane < b_lane)
    before_column = count_by((a_lane < b_lane) & same_column)
    whole = jnp.sum(mask, axis=1, keepdims=True) + jnp.zeros((8, 128), jnp.float32)
    own_column = count_by(same_column)
    rank_y_rows, rank_x_rows = [], []
    for s in range(8):
        ry = before_all[s : s + 1]
        if s % 2 == 1:
            ry = ry + whole[s - 1 : s]
        rx = before_column[s : s + 1]
        for t in range(s % 2, s, 2):
            rx = rx + own_column[t : t + 1]
        rank_y_rows.append(ry)
        rank_x_rows.append(rx)
    rank_y = jnp.concatenate(rank_y_rows, axis=0)
    rank_x = jnp.concatenate(rank_x_rows, axis=0)
    load = jnp.zeros((1, 1), jnp.float32)
    for g in range(4):
        in_y = jnp.where(lax.div(sub, 2) == g, mask, 0.0)
        in_x = jnp.where(lax.rem(sub, 2) * 2 + lax.div(lane, 64) == g, mask, 0.0)
        load = jnp.maximum(load, jnp.sum(in_y, axis=(0, 1), keepdims=True))
        load = jnp.maximum(load, jnp.sum(in_x, axis=(0, 1), keepdims=True))
    info[0] = jnp.where(used, rank_y, -1.0)
    info[1] = jnp.where(used, rank_x, -1.0)
    info[2] = mask
    info[3] = load + jnp.zeros((8, 128), jnp.float32)

    token[0] = jnp.where(used, rank_y, -1.0)
    swapped = lax.rem(x, 2) == 1
    for q, value in ((1, jnp.where(used, rank_x, -1.0)), (2, weight)):
        rolled = pltpu.roll(value, 64, 1)
        token[q] = jnp.where(swapped, rolled, value)
        token[q + 2] = jnp.where(swapped, value, rolled)

    def y_row(q):
        return jnp.concatenate(
            [token[q, pl.ds(2 * y, 1), :], token[q, pl.ds(2 * y + 1, 1), :]], axis=1
        )

    def x_row(q):
        low = lax.broadcasted_iota(jnp.int32, (1, 128), 1) < 64
        half_x = lax.div(x, 2)
        parts = [
            jnp.where(
                low,
                token[q, pl.ds(2 * t + half_x, 1), :],
                token[q + 2, pl.ds(2 * t + 2 + half_x, 1), :],
            )
            for t in (0, 2)
        ]
        return jnp.concatenate(parts, axis=1)

    target = lax.broadcasted_iota(jnp.int32, (256, 256), 0).astype(jnp.float32)
    pick_rows = jnp.where(target == y_row(0), 1.0, 0.0).astype(jnp.bfloat16)
    chosen = target == x_row(1)
    pick_cots = jnp.where(chosen, 1.0, 0.0).astype(jnp.bfloat16)
    row_weight = jnp.sum(jnp.where(chosen, x_row(2), 0.0), axis=1, keepdims=True)

    for a in (0, 1):
        for way in (0, 1):
            origin = turn(pos[a], 3 if way == 0 else 1)
            for block in range(4):
                if block % 2 != way:
                    arrived(got.at[a, origin, block], data_recv.at[a, origin, block])
        origin = turn(pos[a], 2)
        for block in range(4):
            arrived(got.at[a, origin, block], data_recv.at[a, origin, block])

    for part in range(7):
        cols = slice(part * 384, (part + 1) * 384)
        block = got[0, :, :, :, cols].reshape(256, 384)
        out_rows[:, cols] = jnp.dot(
            pick_rows, block, preferred_element_type=jnp.float32
        ).astype(jnp.bfloat16)
        block = got[1, :, :, :, cols].reshape(256, 384)
        packed = jnp.dot(pick_cots, block, preferred_element_type=jnp.float32)
        out_cots[:, cols] = (packed * row_weight).astype(jnp.bfloat16)

    for copy in copies:
        copy.wait_send()

    @pl.when(role == 0)
    def _():
        for copy in column_copies():
            copy.wait_send()

    @pl.when(role == 1)
    def _():
        for k, block in enumerate(blocks):
            handed_on(block, k).wait_send()


def pack(*operands):
    vmem = pl.BlockSpec(memory_space=pltpu.VMEM)
    queries, new_keys, cache_keys = operands[7], operands[8], operands[10]
    return pl.pallas_call(
        pack_kernel,
        out_shape=(
            jax.ShapeDtypeStruct(queries.shape, jnp.bfloat16),
            jax.ShapeDtypeStruct((256, HALF), jnp.bfloat16),
            jax.ShapeDtypeStruct((256, HALF), jnp.bfloat16),
            jax.ShapeDtypeStruct((4, 8, 128), jnp.float32),
        ),
        in_specs=[pl.BlockSpec(memory_space=pltpu.HBM)] * len(operands),
        out_specs=(vmem, vmem, vmem, vmem),
        scratch_shapes=[
            pltpu.SMEM((1,), jnp.int32),
            pltpu.SMEM((4,), jnp.float32),
            pltpu.SMEM((4,), jnp.int32),
            pltpu.SMEM((4,), jnp.int32),
            pltpu.SMEM((4,), jnp.int32),
            pltpu.VMEM((4, 4, D), jnp.bfloat16),
            pltpu.VMEM((4, 4, D), jnp.bfloat16),
            pltpu.VMEM(queries.shape, jnp.bfloat16),
            pltpu.VMEM(new_keys.shape, jnp.bfloat16),
            pltpu.VMEM(new_keys.shape, jnp.bfloat16),
            pltpu.VMEM(cache_keys.shape, jnp.bfloat16),
            pltpu.VMEM(cache_keys.shape, jnp.bfloat16),
            pltpu.VMEM((64, CL), jnp.float32),
            pltpu.VMEM((64, CL), jnp.float32),
            pltpu.VMEM((64, HEAD_DIM), jnp.float32),
            pltpu.SemaphoreType.DMA((10,)),
            pltpu.SemaphoreType.DMA((4, 2)),
            pltpu.VMEM((2, 2, TOK, HALF), jnp.bfloat16),
            pltpu.VMEM((2, 4, 4, TOK, HALF), jnp.bfloat16),
            pltpu.VMEM((4, 4, 4, 8, 128), jnp.float32),
            pltpu.VMEM((5, 8, 128), jnp.float32),
            pltpu.SemaphoreType.DMA((7, 3)),
            pltpu.SemaphoreType.DMA((2, 2, 6)),
            pltpu.SemaphoreType.DMA((2, 4, 4)),
            pltpu.SemaphoreType.DMA((4,)),
            pltpu.SemaphoreType.DMA((3,)),
            pltpu.SemaphoreType.DMA((4,)),
            pltpu.SemaphoreType.DMA((3,)),
            pltpu.SemaphoreType.DMA((4,)),
        ],
        compiler_params=pltpu.CompilerParams(
            collective_id=1, has_side_effects=True, vmem_limit_bytes=62 * 1024 * 1024
        ),
    )(*operands)


PARTS = 4
EDGE = 768
WIDE = HALF - EDGE
ORDER = ((0, 1, 2, 3), (1, 0, 3, 2))


def forward_kernel(
    cap, packed_rows, packed_cots, info, w_gate, w_up, w_down,
    d_gate, d_up, hidden, out_rows, out_cots,
    held, weights, acc, back, row_hot, cot_hot, perm,
    own_send, relay_send, pass_send, z_send, zpass_send,
    ring_recv, pair_recv, z_recv, zpair_recv, local_sem, result_sem,
):
    role, high, x, y, core = place()
    pos = (y, x)
    rows = cap // PARTS
    other = flip(core, 1)
    sibling = device(role, high, x, y, other)
    neighbour = (
        (device(role, high, x, turn(y, 1), core), device(role, high, x, turn(y, 3), core)),
        (device(role, high, turn(x, 1), y, core), device(role, high, turn(x, 3), y, core)),
    )
    across = [device(flip(role, 1), h, x, y, core) for h in (0, 1)]
    carried = pl.ds(pl.multiple_of(role * EDGE, 128), WIDE)
    lent = pl.ds(pl.multiple_of(role * WIDE, 128), EDGE)
    foreign = pl.ds(pl.multiple_of((1 - role) * WIDE, 128), EDGE)
    source = (packed_rows, packed_cots)
    local = [
        pltpu.make_async_copy(source[a].at[pl.ds(0, cap)], held.at[a, core, 0], local_sem.at[a])
        for a in (0, 1)
    ] + [
        pltpu.make_async_copy(w, weights.at[i], local_sem.at[2 + i])
        for i, w in enumerate((w_gate, w_up, w_down))
    ]
    for copy in local:
        copy.start()
    meet([sibling, *neighbour[0], *neighbour[1], *across])

    copies = []

    def part_of(index):
        return lax.rem(index + 2 * high, PARTS)

    def piece(part, count=1):
        return pl.ds(pl.multiple_of(part * rows, rows), rows * count)

    def send(src, dst, send_sem, recv_sem, target):
        copy = remote(dst if src is None else src, dst, send_sem, recv_sem, target)
        copy.start()
        copies.append(copy)

    def arrived(ref, sem):
        remote(ref, ref, sem, sem, sibling).wait_recv()

    for i in range(PARTS):
        for a in (0, 1):
            for way in (0, 1):
                part = part_of(ORDER[way][i])
                send(
                    source[a].at[piece(part), carried],
                    held.at[a, core, 1 + way, piece(part), carried],
                    own_send.at[a, way, i], ring_recv.at[a, 1 + way, part], neighbour[a][way],
                )
            part = part_of(i)
            send(
                source[a].at[piece(part)], held.at[a, core, 0, piece(part)],
                own_send.at[a, 2, i], pair_recv.at[a, 0, part], sibling,
            )

    def lend(a, slot, index):
        part = part_of(index)
        for h in (0, 1):
            ref = held.at[a, core, slot, piece(part), lent]
            send(None, ref, z_send.at[a, slot, index, h], z_recv.at[a, slot, part], across[h])

    def hand(a, slot, index):
        part = part_of(index)
        ref = held.at[a, core, slot, piece(part), carried]
        send(None, ref, pass_send.at[a, slot, index], pair_recv.at[a, slot, part], sibling)

    def beside(i):
        for a in (0, 1):
            for way in (0, 1):
                index = ORDER[way][i]
                part = part_of(index)
                ref = held.at[a, core, 1 + way, piece(part), carried]
                arrived(ref, ring_recv.at[a, 1 + way, part])
                if i % 2 == 0:
                    send(
                        ref, held.at[a, core, 3, piece(part), carried],
                        relay_send.at[a, way, i // 2], ring_recv.at[a, 3, part], neighbour[a][way],
                    )
                if index < 2:
                    lend(a, 1 + way, index)
        for a in (0, 1):
            for way in (0, 1):
                hand(a, 1 + way, ORDER[way][i])

    def opposite(index):
        for a in (0, 1):
            part = part_of(index)
            arrived(held.at[a, core, 3, piece(part), carried], ring_recv.at[a, 3, part])
            if index < 2:
                lend(a, 3, index)
        for a in (0, 1):
            hand(a, 3, index)

    def borrowed(slot):
        for h in (0, 1):
            for a in (0, 1):
                for part in (2 * h, 2 * h + 1):
                    arrived(held.at[a, core, slot, piece(part), foreign], z_recv.at[a, slot, part])
                ref = held.at[a, core, slot, piece(2 * h, 2), foreign]
                send(None, ref, zpass_send.at[a, slot, h], zpair_recv.at[a, slot, h], sibling)

    def paired(slot):
        for a in (0, 1):
            for part in range(PARTS):
                arrived(held.at[a, other, slot, piece(part), carried], pair_recv.at[a, slot, part])

    def zpaired(slot):
        for a in (0, 1):
            for h in (0, 1):
                arrived(
                    held.at[a, other, slot, piece(2 * h, 2), foreign], zpair_recv.at[a, slot, h]
                )

    def product(which, slot, count):
        a = 0 if which < 2 else 1
        total = None
        for half in (0, 1):
            term = lax.dot_general(
                weights[which, :, half * HALF : (half + 1) * HALF],
                held[a, half, slot : slot + count].reshape(count * cap, HALF),
                NT,
                preferred_element_type=jnp.float32,
            )
            total = term if total is None else total + term
        acc[which, :, slot * cap : (slot + count) * cap] = total

    def partial(slot, half, start, width, first=False):
        cols = slice(slot * cap, (slot + 1) * cap)
        for which in range(3):
            term = lax.dot_general(
                weights[which, :, pl.ds(pl.multiple_of(half * HALF + start, 128), width)],
                held[0 if which < 2 else 1, half, slot, :, pl.ds(pl.multiple_of(start, 128), width)],
                NT,
                preferred_element_type=jnp.float32,
            )
            acc[which, :, cols] = term if first else acc[which, :, cols] + term

    def slot_of(line, here):
        step = lax.rem(line - here + 4, 4)
        return jnp.where(
            step == 0, 0.0, jnp.where(step == 3, 1.0, jnp.where(step == 1, 2.0, 3.0))
        )

    lane = lax.broadcasted_iota(jnp.int32, (1, 128), 1)
    place_at = lax.broadcasted_iota(jnp.int32, (4 * cap, 128), 0).astype(jnp.float32)
    for s in range(8):
        cols = slice(s * 128, (s + 1) * 128)
        used = info[2, s : s + 1, :] > 0.0
        in_rows = info[0, s : s + 1, :] + slot_of(s // 2, y) * float(cap)
        in_cots = info[1, s : s + 1, :] + slot_of(lax.div(lane, 64) + (s % 2) * 2, x) * float(cap)
        in_rows = jnp.where(used, in_rows, -1.0)
        in_cots = jnp.where(used, in_cots, -1.0)
        row_hot[:, cols] = jnp.where(place_at == in_rows, 1.0, 0.0).astype(jnp.bfloat16)
        cot_hot[:, cols] = jnp.where(place_at == in_cots, 1.0, 0.0).astype(jnp.bfloat16)

    beside(0)

    @pl.loop(0, 4 * cap // 128)
    def _(i):
        some = pl.ds(pl.multiple_of(i * 128, 128), 128)
        perm[some, :] = lax.dot_general(
            cot_hot[some, :], row_hot[...], NT, preferred_element_type=jnp.float32
        ).astype(jnp.bfloat16)

    beside(1)

    def finish(slot, count):
        cols = slice(slot * cap, (slot + count) * cap)
        up = acc[1, :, cols]
        active, slope = gelu_pair(acc[0, :, cols])
        acc[0, :, cols] = active
        acc[1, :, cols] = up * slope
        row_hot[0:HID, cols] = (active * up).astype(jnp.bfloat16)

    def spread(slot, count):
        some = slice(slot * cap, (slot + count) * cap)
        term = acc[2, :, some]
        upper = term.astype(jnp.bfloat16)
        lower = (term - upper.astype(jnp.float32)).astype(jnp.bfloat16)
        for i in range(4 * cap // 256):
            cols = slice(i * 256, (i + 1) * 256)
            moved = jnp.dot(upper, perm[some, cols], preferred_element_type=jnp.float32) + jnp.dot(
                lower, perm[some, cols], preferred_element_type=jnp.float32
            )
            back[:, cols] = moved if slot == 0 else back[:, cols] + moved

    def results(slot, count):
        return [
            pltpu.make_async_copy(
                held.at[a, role, pl.ds(slot, count)],
                out.at[pl.ds(slot, count)],
                result_sem.at[a, slot // 3],
            )
            for a, out in ((0, out_rows), (1, out_cots))
        ]

    for copy in local:
        copy.wait()
    for a in (0, 1):
        for part in range(PARTS):
            arrived(held.at[a, other, 0, piece(part)], pair_recv.at[a, 0, part])
    for which in range(3):
        product(which, 0, 1)
    beside(2)
    beside(3)
    finish(0, 1)
    opposite(0)
    opposite(1)
    spread(0, 1)
    for slot in (1, 2):
        borrowed(slot)
    for slot in (1, 2):
        paired(slot)
    for slot in (1, 2):
        zpaired(slot)
    for copy in results(0, 3):
        copy.start()
    product(0, 1, 2)
    product(1, 1, 2)
    opposite(2)
    opposite(3)
    product(2, 1, 2)
    finish(1, 2)
    borrowed(3)
    spread(1, 2)
    partial(3, core, role * EDGE, WIDE, True)
    partial(3, core, (1 - role) * WIDE, EDGE)
    paired(3)
    partial(3, other, role * EDGE, WIDE)
    zpaired(3)
    for copy in results(3, 1):
        copy.start()
    partial(3, other, (1 - role) * WIDE, EDGE)
    finish(3, 1)
    spread(3, 1)
    for i in range(4 * cap // 128):
        cols = slice(i * 128, (i + 1) * 128)
        d_up[:, cols] = (back[:, cols] * acc[0, :, cols]).astype(jnp.bfloat16)
        d_gate[:, cols] = (back[:, cols] * acc[1, :, cols]).astype(jnp.bfloat16)
    for i in range(4 * cap // 256):
        cols = slice(i * 256, (i + 1) * 256)
        hidden[:, cols] = lax.dot_general(
            row_hot[0:HID, 0 : 4 * cap], perm[cols, :], NT, preferred_element_type=jnp.float32
        ).astype(jnp.bfloat16)

    for copy in copies:
        copy.wait_send()
    for copy in results(0, 3) + results(3, 1):
        copy.wait()


def forward(cap, packed_rows, packed_cots, info, w_gate, w_up, w_down):
    vmem = pl.BlockSpec(memory_space=pltpu.VMEM)
    hbm = pl.BlockSpec(memory_space=pltpu.HBM)
    small = jax.ShapeDtypeStruct((HID, 4 * cap), jnp.bfloat16)
    large = jax.ShapeDtypeStruct((4, cap, HALF), jnp.bfloat16)
    d_gate, d_up, hidden, rows, cots = pl.pallas_call(
        functools.partial(forward_kernel, cap),
        out_shape=(small, small, small, large, large),
        in_specs=[hbm, hbm, vmem, hbm, hbm, hbm],
        out_specs=(vmem, vmem, vmem, hbm, hbm),
        scratch_shapes=[
            pltpu.VMEM((2, 2, 4, cap, HALF), jnp.bfloat16),
            pltpu.VMEM((3, HID, D), jnp.bfloat16),
            pltpu.VMEM((3, HID, 4 * cap), jnp.float32),
            pltpu.VMEM((HID, 4 * cap), jnp.float32),
            pltpu.VMEM((4 * cap, 1024), jnp.bfloat16),
            pltpu.VMEM((4 * cap, 1024), jnp.bfloat16),
            pltpu.VMEM((4 * cap, 4 * cap), jnp.bfloat16),
            pltpu.SemaphoreType.DMA((2, 3, 4)),
            pltpu.SemaphoreType.DMA((2, 2, 2)),
            pltpu.SemaphoreType.DMA((2, 4, 4)),
            pltpu.SemaphoreType.DMA((2, 4, 2, 2)),
            pltpu.SemaphoreType.DMA((2, 4, 2)),
            pltpu.SemaphoreType.DMA((2, 4, 4)),
            pltpu.SemaphoreType.DMA((2, 4, 4)),
            pltpu.SemaphoreType.DMA((2, 4, 4)),
            pltpu.SemaphoreType.DMA((2, 4, 2)),
            pltpu.SemaphoreType.DMA((5,)),
            pltpu.SemaphoreType.DMA((2, 2)),
        ],
        compiler_params=pltpu.CompilerParams(
            collective_id=2 if cap == 128 else 3,
            has_side_effects=True,
            vmem_limit_bytes=62 * 1024 * 1024,
        ),
    )(packed_rows, packed_cots, info, w_gate, w_up, w_down)
    rows = rows.reshape(4 * cap, HALF)
    cots = cots.reshape(4 * cap, HALF)
    tile = 896
    whole = pl.BlockSpec((HID, 4 * cap), lambda i: (0, 0))
    tall = pl.BlockSpec((4 * cap, tile), lambda i: (0, i))
    wide = pl.BlockSpec((HID, tile), lambda i: (0, i))
    return pl.pallas_call(
        gradient_kernel,
        grid=(HALF // tile,),
        out_shape=(jax.ShapeDtypeStruct((HID, HALF), jnp.bfloat16),) * 3,
        in_specs=[whole, whole, whole, tall, tall],
        out_specs=(wide, wide, wide),
        compiler_params=pltpu.CompilerParams(vmem_limit_bytes=62 * 1024 * 1024),
    )(d_gate, d_up, hidden, rows, cots)


def gradient_kernel(d_gate, d_up, hidden, rows, cots, grad_gate, grad_up, grad_down):
    for left, right, out in (
        (d_gate, rows, grad_gate),
        (d_up, rows, grad_up),
        (hidden, cots, grad_down),
    ):
        out[...] = jnp.dot(left[...], right[...], preferred_element_type=jnp.float32).astype(
            jnp.bfloat16
        )


def local(
    queries, new_keys, new_values, cache_keys, cache_values, context_lengths,
    rollout_rows, cotangents, rewards, prompt_keys, completion_lengths, finished_counts,
    gate_weight, up_weight, down_weight,
):
    attended, packed_rows, packed_cots, info = pack(
        finished_counts, rewards, prompt_keys, completion_lengths, context_lengths,
        rollout_rows, cotangents, queries, new_keys, new_values, cache_keys, cache_values,
    )
    operands = (packed_rows, packed_cots, info, gate_weight.T, up_weight.T, down_weight)
    grad_gate, grad_up, grad_down = lax.cond(
        info[3, 0, 0] <= 128.0,
        functools.partial(forward, 128),
        functools.partial(forward, 256),
        *operands,
    )
    return (attended, grad_gate.T, grad_up.T, grad_down)


def solution(mesh):
    return jax.shard_map(
        local,
        mesh=mesh,
        in_specs=(
            P("fsdp", None, None),
            P("fsdp", None, None),
            P("fsdp", None, None),
            P("fsdp", None, None),
            P("fsdp", None, None),
            P("fsdp"),
            P(("role", "fsdp"), None, None),
            P(("role", "fsdp"), None, None),
            P(("role", "fsdp")),
            P(("role", "fsdp")),
            P(("role", "fsdp")),
            P(("role", "fsdp")),
            P(None, "fsdp"),
            P(None, "fsdp"),
            P("fsdp", None),
        ),
        out_specs=(P("fsdp", None, None), P("role", "fsdp"), P("role", "fsdp"), P("fsdp", "role")),
        check_vma=False,
    )
```

```python
import functools

import jax
import jax.numpy as jnp
from jax import lax
from jax.experimental import pallas as pl
from jax.experimental.pallas import tpu as pltpu
from jax.sharding import PartitionSpec as P

HEADS = 32
KV_HEADS = 16
HEAD_DIM = 128
QSCALAR = 168
GROUP = 16
GROUPS = 8
CL = 256
D = 5376
HALF = 2688
HID = 336
TOK = 16
MESH = pl.DeviceIdType.MESH
NT = (((1,), (1,)), ((), ()))


def gelu_pair(values):
    inner_arg = 0.7978845608028654 * (values + 0.044715 * values * values * values)
    tangent = jnp.tanh(inner_arg)
    result = 0.5 * values * (1.0 + tangent)
    slope_value = 0.5 * (1.0 + tangent) + 0.5 * values * (
        1.0 - tangent * tangent
    ) * 0.7978845608028654 * (1.0 + 3.0 * 0.044715 * values * values)
    return (result, slope_value)


def attend_sample(s, valid, query, fresh_key, fresh_value, keys, values, out, scores, probs, mixed):
    scale = float(QSCALAR) ** (-0.5)

    def stack(ref, count):
        wide = ref[s].astype(jnp.float32)
        parts = [wide[:, j * HEAD_DIM : (j + 1) * HEAD_DIM] for j in range(count)]
        return jnp.concatenate(parts, axis=0)

    asked = stack(query, HEADS)
    new_keys = stack(fresh_key, KV_HEADS).astype(jnp.bfloat16)
    new_values = stack(fresh_value, KV_HEADS).astype(jnp.bfloat16)
    for k in range(KV_HEADS):
        scores[4 * k : 4 * k + 4, :] = lax.dot_general(
            asked[4 * k : 4 * k + 4].astype(jnp.bfloat16),
            keys[s, :, k * HEAD_DIM : (k + 1) * HEAD_DIM],
            NT,
            preferred_element_type=jnp.float32,
        )
    fresh = lax.dot_general(
        asked.astype(jnp.bfloat16), new_keys, NT, preferred_element_type=jnp.float32
    )
    row = lax.broadcasted_iota(jnp.int32, (64, 32), 0)
    column = lax.broadcasted_iota(jnp.int32, (64, 32), 1)
    seen = (lax.div(row, 4) == lax.div(column, 2)) & (lax.rem(column, 2) <= lax.rem(row, 2))
    fresh = jnp.where(seen, fresh * scale, -1e30)
    position = lax.broadcasted_iota(jnp.int32, (64, CL), 1)
    cached = jnp.where(position < valid, scores[...] * scale, -1e30)
    top = jnp.maximum(
        jnp.max(cached, axis=-1, keepdims=True), jnp.max(fresh, axis=-1, keepdims=True)
    )
    cached = jnp.exp(cached - top)
    fresh = jnp.exp(fresh - top)
    total = jnp.sum(cached, axis=-1, keepdims=True) + jnp.sum(fresh, axis=-1, keepdims=True)
    probs[...] = cached / total
    fresh = (fresh / total).astype(jnp.bfloat16)
    mixed[...] = jnp.dot(fresh, new_values, preferred_element_type=jnp.float32)
    for k in range(KV_HEADS):
        mixed[4 * k : 4 * k + 4, :] += jnp.dot(
            probs[4 * k : 4 * k + 4, :].astype(jnp.bfloat16),
            values[s, :, k * HEAD_DIM : (k + 1) * HEAD_DIM],
            preferred_element_type=jnp.float32,
        )
    done = mixed[...]
    out[s] = jnp.concatenate(
        [done[2 * j : 2 * j + 2] for j in range(HEADS)], axis=1
    ).astype(jnp.bfloat16)


def place():
    role = lax.axis_index("role")
    index = lax.axis_index("fsdp")
    return (
        role,
        lax.div(index, 32),
        lax.rem(lax.div(index, 8), 4),
        lax.rem(lax.div(index, 2), 4),
        lax.rem(index, 2),
    )


def device(role, high, x, y, core):
    return {"role": role, "fsdp": ((high * 4 + x) * 4 + y) * 2 + core}


def flip(bit, other):
    return lax.rem(bit + other, 2)


def turn(pos, step):
    return lax.rem(pos + step, 4)


def meet(partners):
    barrier = pltpu.get_barrier_semaphore()
    for partner in partners:
        pl.semaphore_signal(barrier, inc=1, device_id=partner, device_id_type=MESH)
    pl.semaphore_wait(barrier, len(partners))


def remote(src, dst, send, recv, target):
    return pltpu.make_async_remote_copy(
        src_ref=src,
        dst_ref=dst,
        send_sem=send,
        recv_sem=recv,
        device_id=target,
        device_id_type=MESH,
    )


def pack_kernel(
    count_in, reward_in, key_in, length_in, context_in, rows_in, cots_in,
    query_in, fresh_key_in, fresh_value_in, keys_in, values_in,
    attended, out_rows, out_cots, info,
    count, reward, key, length, context, rows, cots, query, fresh_key, fresh_value,
    keys, values, scores, probs, mixed, load_sem, cache_sem,
    src, got, meta, token, col_send, ring_send, data_recv,
    mcol_recv, mx_send, mx_recv, my_send, my_recv,
):
    role, high, x, y, core = place()
    mine = high * 2 + core
    pos = (x, y)
    offsets = [(dr, dh, dc) for dr in (0, 1) for dh in (0, 1) for dc in (0, 1)][1:]
    column = [
        device(flip(role, dr), flip(high, dh), x, y, flip(core, dc)) for dr, dh, dc in offsets
    ]
    x_line = [device(role, high, turn(x, s), y, core) for s in (1, 2, 3)]
    y_line = [device(role, high, x, turn(y, s), core) for s in (1, 2, 3)]
    line = (x_line, y_line)
    neighbour = ((x_line[0], x_line[2]), (y_line[0], y_line[2]))
    loads = [
        pltpu.make_async_copy(a, b, load_sem.at[i])
        for i, (a, b) in enumerate(
            (
                (count_in, count), (reward_in, reward), (key_in, key), (length_in, length),
                (rows_in, rows), (cots_in, cots), (context_in, context), (query_in, query),
                (fresh_key_in, fresh_key), (fresh_value_in, fresh_value),
            )
        )
    ]
    caches = [
        [
            pltpu.make_async_copy(a.at[s], b.at[s], cache_sem.at[s, i])
            for i, (a, b) in enumerate(((keys_in, keys), (values_in, values)))
        ]
        for s in range(4)
    ]
    for copy in loads:
        copy.start()

    def attend(s):
        for copy in caches[s]:
            copy.wait()
        attend_sample(
            s, context[s], query, fresh_key, fresh_value, keys, values, attended,
            scores, probs, mixed,
        )

    for copy in loads[:6]:
        copy.wait()
    meet(column + x_line + y_line)

    copies = []

    def send(src_ref, dst_ref, send_sem, recv_sem, target):
        copy = remote(src_ref, dst_ref, send_sem, recv_sem, target)
        copy.start()
        return copy

    def arrived(ref, sem):
        remote(ref, ref, sem, sem, x_line[0]).wait_recv()

    def column_copies():
        made = []
        for i, (dr, dh, dc) in enumerate(offsets):
            made.append(
                remote(
                    meta.at[y, x, mine], meta.at[y, x, mine],
                    col_send.at[i, 2], mcol_recv.at[mine], column[i],
                )
            )
        for step in (0, 1):
            for i, (dr, dh, dc) in enumerate(offsets):
                if dr == 0 and dh == 1:
                    continue
                part = flip(core, dc)
                a = flip(high, dh + step)
                spot = jnp.where(a == 0, x, y)
                made.append(
                    remote(
                        src.at[a, part], got.at[a, spot, mine],
                        col_send.at[i, a], data_recv.at[a, spot, mine], column[i],
                    )
                )
        return made

    lane = lax.broadcasted_iota(jnp.int32, (8, 128), 1)
    sub = lax.broadcasted_iota(jnp.int32, (8, 128), 0)

    @pl.when(role == 0)
    def _():
        base = (lax.rem(x, 2) * 4 + mine) * TOK
        tile = jnp.zeros((8, 128), jnp.float32)
        for s in range(4):
            here = (lane >= base + 4 * s) & (lane < base + 4 * s + 4)
            live = jnp.where(s < count[0], 1.0, 0.0)
            value = jnp.where(
                sub == 0,
                reward[s],
                jnp.where(
                    sub == 1,
                    key[s].astype(jnp.float32),
                    jnp.where(
                        sub == 2,
                        length[s].astype(jnp.float32),
                        jnp.where(sub == 3, live, 0.0),
                    ),
                ),
            )
            tile = jnp.where(here, value, tile)
        meta[y, x, mine] = tile
        for a, ref in enumerate((rows, cots)):
            wide = jnp.concatenate(
                [ref[s].astype(jnp.float32) for s in range(4)], axis=0
            ).astype(jnp.bfloat16)
            src[a, 0] = wide[:, :HALF]
            src[a, 1] = wide[:, HALF:]
        for copy in column_copies():
            copy.start()
        for a in (0, 1):
            got[a, pos[a], mine] = src[a, core]

    for pair in caches:
        for copy in pair:
            copy.start()
    for copy in loads[6:]:
        copy.wait()

    blocks = [
        flip(high, dh) * 2 + flip(core, dc) for dh, dc in ((0, 0), (0, 1), (1, 0), (1, 1))
    ]

    def spot_of(a):
        return jnp.where(a == 0, x, y)

    def beside(a, way):
        step = 1 if way == 0 else 3
        return device(
            role, high, jnp.where(a == 0, turn(x, step), x), jnp.where(a == 0, y, turn(y, step)), core
        )

    def handed_on(k):
        block = blocks[k]
        here = got.at[high, spot_of(high), block]
        return remote(
            here, here, col_send.at[k, 0], data_recv.at[high, spot_of(high), block],
            device(0, flip(lax.div(block, 2), 1), x, y, core),
        )

    def from_column(a, k, wait=True, hand=False):
        block = blocks[k]
        here = got.at[a, spot_of(a), block]
        sem = data_recv.at[a, spot_of(a), block]
        if wait:
            arrived(here, sem)
        if hand:
            handed_on(k).start()
        for way in (0, 1):
            remote(here, here, ring_send.at[a, way, k], sem, beside(a, way)).start()

    def relay(a, i):
        for way in (0, 1):
            origin = turn(spot_of(a), 3 if way == 0 else 1)
            block = 2 * flip(high, i) + way
            here = got.at[a, origin, block]
            sem = data_recv.at[a, origin, block]
            arrived(here, sem)
            remote(here, here, ring_send.at[a, way, 4 + i], sem, beside(a, way)).start()

    def wait_column(k, what):
        if k == 0:
            @pl.when(role == 1)
            def _():
                what()
        else:
            what()

    @pl.when(role == 0)
    def _():
        for k in (0, 1):
            for a in (0, 1):
                from_column(a, k, wait=k > 0)

    @pl.when(role == 1)
    def _():
        for k in range(4):
            from_column(high, k, hand=True)

    for k, block in enumerate(blocks):
        wait_column(
            k, lambda block=block: arrived(meta.at[y, x, block], mcol_recv.at[block])
        )
    for i in range(3):
        copies.append(
            send(meta.at[y, x], meta.at[y, x], mx_send.at[i], mx_recv.at[x], x_line[i])
        )

    @pl.when(role == 0)
    def _():
        for a in (0, 1):
            relay(a, 0)
        for k in (2, 3):
            for a in (0, 1):
                from_column(a, k)

    @pl.when(role == 1)
    def _():
        for i in (0, 1):
            for k in (2 * i, 2 * i + 1):
                from_column(1 - high, k)
            relay(high, i)

    for i in (1, 2, 3):
        other = turn(x, i)
        arrived(meta.at[y, other], mx_recv.at[other])
    for i in range(3):
        copies.append(send(meta.at[y], meta.at[y], my_send.at[i], my_recv.at[y], y_line[i]))

    @pl.when(role == 0)
    def _():
        for a in (0, 1):
            relay(a, 1)

    @pl.when(role == 1)
    def _():
        for i in (0, 1):
            relay(1 - high, i)

    attend(0)
    for i in (1, 2, 3):
        other = turn(y, i)
        arrived(meta.at[other], my_recv.at[other])

    attend(1)
    attend(2)
    attend(3)

    tiles = []
    for s in range(8):
        total = jnp.zeros((8, 128), jnp.float32)
        for xi in (0, 1):
            for block in range(4):
                total = total + meta[s // 2, (s % 2) * 2 + xi, block]
        tiles.append(total)
    rewards, keys, lengths, live = (
        jnp.concatenate([t[q : q + 1] for t in tiles], axis=0) for q in range(4)
    )
    step = lax.rem(lane, 4).astype(jnp.float32)
    first = jnp.where(step == 0.0, live, 0.0)
    mean = jnp.zeros((8, 128), jnp.float32)
    denominator = jnp.ones((8, 128), jnp.float32)
    for k in range(GROUPS):
        same = keys == float(k)
        member = jnp.where(same, first, 0.0)
        group_sum = jnp.sum(member * rewards, axis=(0, 1), keepdims=True)
        group_sq = jnp.sum(member * (rewards * rewards), axis=(0, 1), keepdims=True)
        group_mean = group_sum / GROUP
        spread = group_sq / GROUP - group_mean * group_mean
        divisor = jnp.maximum(jnp.sqrt(jnp.maximum(spread, 0.0)), 1.0)
        mean = jnp.where(same, group_mean, mean)
        denominator = jnp.where(same, divisor, denominator)
    used = (live > 0.0) & (step < lengths)
    mask = jnp.where(used, 1.0, 0.0)
    weight = jnp.where(used, (rewards - mean) / denominator / jnp.maximum(lengths, 1.0), 0.0)

    a_lane = lax.broadcasted_iota(jnp.int32, (128, 128), 0)
    b_lane = lax.broadcasted_iota(jnp.int32, (128, 128), 1)
    same_column = (a_lane < 64) == (b_lane < 64)

    def count_by(take):
        return jnp.dot(
            mask.astype(jnp.bfloat16),
            jnp.where(take, 1.0, 0.0).astype(jnp.bfloat16),
            preferred_element_type=jnp.float32,
        )

    before_all = count_by(a_lane < b_lane)
    before_column = count_by((a_lane < b_lane) & same_column)
    whole = jnp.sum(mask, axis=1, keepdims=True) + jnp.zeros((8, 128), jnp.float32)
    own_column = count_by(same_column)
    rank_y_rows, rank_x_rows = [], []
    for s in range(8):
        ry = before_all[s : s + 1]
        if s % 2 == 1:
            ry = ry + whole[s - 1 : s]
        rx = before_column[s : s + 1]
        for t in range(s % 2, s, 2):
            rx = rx + own_column[t : t + 1]
        rank_y_rows.append(ry)
        rank_x_rows.append(rx)
    rank_y = jnp.concatenate(rank_y_rows, axis=0)
    rank_x = jnp.concatenate(rank_x_rows, axis=0)
    load = jnp.zeros((1, 1), jnp.float32)
    for g in range(4):
        in_y = jnp.where(lax.div(sub, 2) == g, mask, 0.0)
        in_x = jnp.where(lax.rem(sub, 2) * 2 + lax.div(lane, 64) == g, mask, 0.0)
        load = jnp.maximum(load, jnp.sum(in_y, axis=(0, 1), keepdims=True))
        load = jnp.maximum(load, jnp.sum(in_x, axis=(0, 1), keepdims=True))
    info[0] = jnp.where(used, rank_y, -1.0)
    info[1] = jnp.where(used, rank_x, -1.0)
    info[2] = mask
    info[3] = load + jnp.zeros((8, 128), jnp.float32)

    token[0] = jnp.where(used, rank_y, -1.0)
    swapped = lax.rem(x, 2) == 1
    for q, value in ((1, jnp.where(used, rank_x, -1.0)), (2, weight)):
        rolled = pltpu.roll(value, 64, 1)
        token[q] = jnp.where(swapped, rolled, value)
        token[q + 2] = jnp.where(swapped, value, rolled)

    def y_row(q):
        return jnp.concatenate(
            [token[q, pl.ds(2 * y, 1), :], token[q, pl.ds(2 * y + 1, 1), :]], axis=1
        )

    def x_row(q):
        low = lax.broadcasted_iota(jnp.int32, (1, 128), 1) < 64
        half_x = lax.div(x, 2)
        parts = [
            jnp.where(
                low,
                token[q, pl.ds(2 * t + half_x, 1), :],
                token[q + 2, pl.ds(2 * t + 2 + half_x, 1), :],
            )
            for t in (0, 2)
        ]
        return jnp.concatenate(parts, axis=1)

    target = lax.broadcasted_iota(jnp.int32, (256, 256), 0).astype(jnp.float32)
    pick_rows = jnp.where(target == y_row(0), 1.0, 0.0).astype(jnp.bfloat16)
    chosen = target == x_row(1)
    pick_cots = jnp.where(chosen, 1.0, 0.0).astype(jnp.bfloat16)
    row_weight = jnp.sum(jnp.where(chosen, x_row(2), 0.0), axis=1, keepdims=True)

    for a in (0, 1):
        for way in (0, 1):
            origin = turn(pos[a], 3 if way == 0 else 1)
            for block in range(4):
                if block % 2 != way:
                    arrived(got.at[a, origin, block], data_recv.at[a, origin, block])
        origin = turn(pos[a], 2)
        for block in range(4):
            arrived(got.at[a, origin, block], data_recv.at[a, origin, block])

    for part in range(7):
        cols = slice(part * 384, (part + 1) * 384)
        block = got[0, :, :, :, cols].reshape(256, 384)
        out_rows[:, cols] = jnp.dot(
            pick_rows, block, preferred_element_type=jnp.float32
        ).astype(jnp.bfloat16)
        block = got[1, :, :, :, cols].reshape(256, 384)
        packed = jnp.dot(pick_cots, block, preferred_element_type=jnp.float32)
        out_cots[:, cols] = (packed * row_weight).astype(jnp.bfloat16)

    for copy in copies:
        copy.wait_send()
    for a in (0, 1):
        for way in (0, 1):
            for k in range(6):
                here = got.at[a, pos[a], mine]
                sem = ring_send.at[a, way, k]
                remote(here, here, sem, sem, beside(a, way)).wait_send()

    @pl.when(role == 0)
    def _():
        for copy in column_copies():
            copy.wait_send()

    @pl.when(role == 1)
    def _():
        for k in range(4):
            handed_on(k).wait_send()


def pack(*operands):
    vmem = pl.BlockSpec(memory_space=pltpu.VMEM)
    queries, new_keys, cache_keys = operands[7], operands[8], operands[10]
    return pl.pallas_call(
        pack_kernel,
        out_shape=(
            jax.ShapeDtypeStruct(queries.shape, jnp.bfloat16),
            jax.ShapeDtypeStruct((256, HALF), jnp.bfloat16),
            jax.ShapeDtypeStruct((256, HALF), jnp.bfloat16),
            jax.ShapeDtypeStruct((4, 8, 128), jnp.float32),
        ),
        in_specs=[pl.BlockSpec(memory_space=pltpu.HBM)] * len(operands),
        out_specs=(vmem, vmem, vmem, vmem),
        scratch_shapes=[
            pltpu.SMEM((1,), jnp.int32),
            pltpu.SMEM((4,), jnp.float32),
            pltpu.SMEM((4,), jnp.int32),
            pltpu.SMEM((4,), jnp.int32),
            pltpu.SMEM((4,), jnp.int32),
            pltpu.VMEM((4, 4, D), jnp.bfloat16),
            pltpu.VMEM((4, 4, D), jnp.bfloat16),
            pltpu.VMEM(queries.shape, jnp.bfloat16),
            pltpu.VMEM(new_keys.shape, jnp.bfloat16),
            pltpu.VMEM(new_keys.shape, jnp.bfloat16),
            pltpu.VMEM(cache_keys.shape, jnp.bfloat16),
            pltpu.VMEM(cache_keys.shape, jnp.bfloat16),
            pltpu.VMEM((64, CL), jnp.float32),
            pltpu.VMEM((64, CL), jnp.float32),
            pltpu.VMEM((64, HEAD_DIM), jnp.float32),
            pltpu.SemaphoreType.DMA((10,)),
            pltpu.SemaphoreType.DMA((4, 2)),
            pltpu.VMEM((2, 2, TOK, HALF), jnp.bfloat16),
            pltpu.VMEM((2, 4, 4, TOK, HALF), jnp.bfloat16),
            pltpu.VMEM((4, 4, 4, 8, 128), jnp.float32),
            pltpu.VMEM((5, 8, 128), jnp.float32),
            pltpu.SemaphoreType.DMA((7, 3)),
            pltpu.SemaphoreType.DMA((2, 2, 6)),
            pltpu.SemaphoreType.DMA((2, 4, 4)),
            pltpu.SemaphoreType.DMA((4,)),
            pltpu.SemaphoreType.DMA((3,)),
            pltpu.SemaphoreType.DMA((4,)),
            pltpu.SemaphoreType.DMA((3,)),
            pltpu.SemaphoreType.DMA((4,)),
        ],
        compiler_params=pltpu.CompilerParams(
            collective_id=1, has_side_effects=True, vmem_limit_bytes=62 * 1024 * 1024
        ),
    )(*operands)


PARTS = 4
EDGE = 896
WIDE = HALF - EDGE
ORDER = ((0, 1, 2, 3), (1, 0, 3, 2))


def forward_kernel(
    cap, packed_rows, packed_cots, info, w_gate, w_up, w_down,
    deltas, out_rows, out_cots,
    held, weights, acc, back, staged, row_hot, cot_hot, perm,
    own_send, relay_send, pass_send, z_send, zpass_send,
    ring_recv, pair_recv, z_recv, zpair_recv, local_sem, result_sem,
):
    role, high, x, y, core = place()
    pos = (y, x)
    rows = cap // PARTS
    other = flip(core, 1)
    sibling = device(role, high, x, y, other)
    neighbour = (
        (device(role, high, x, turn(y, 1), core), device(role, high, x, turn(y, 3), core)),
        (device(role, high, turn(x, 1), y, core), device(role, high, turn(x, 3), y, core)),
    )
    across = [device(flip(role, 1), h, x, y, core) for h in (0, 1)]
    carried = pl.ds(pl.multiple_of(role * EDGE, 128), WIDE)
    lent = pl.ds(pl.multiple_of(role * WIDE, 128), EDGE)
    foreign = pl.ds(pl.multiple_of((1 - role) * WIDE, 128), EDGE)
    source = (packed_rows, packed_cots)
    local = [
        pltpu.make_async_copy(source[a].at[pl.ds(0, cap)], held.at[a, core, 0], local_sem.at[a])
        for a in (0, 1)
    ] + [
        pltpu.make_async_copy(w, weights.at[i], local_sem.at[2 + i])
        for i, w in enumerate((w_gate, w_up, w_down))
    ]
    for copy in local:
        copy.start()
    meet([sibling, *neighbour[0], *neighbour[1], *across])

    copies = []

    def part_of(index):
        return lax.rem(index + 2 * high, PARTS)

    def piece(part, count=1):
        return pl.ds(pl.multiple_of(part * rows, rows), rows * count)

    def send(src, dst, send_sem, recv_sem, target):
        copy = remote(dst if src is None else src, dst, send_sem, recv_sem, target)
        copy.start()
        copies.append(copy)

    def arrived(ref, sem):
        remote(ref, ref, sem, sem, sibling).wait_recv()

    for i in range(PARTS):
        for a in (0, 1):
            for way in (0, 1):
                part = part_of(ORDER[way][i])
                send(
                    source[a].at[piece(part), carried],
                    held.at[a, core, 1 + way, piece(part), carried],
                    own_send.at[a, way, i], ring_recv.at[a, 1 + way, part], neighbour[a][way],
                )
            part = part_of(i)
            send(
                source[a].at[piece(part)], held.at[a, core, 0, piece(part)],
                own_send.at[a, 2, i], pair_recv.at[a, 0, part], sibling,
            )

    def lend(a, slot, index):
        part = part_of(index)
        for h in (0, 1):
            ref = held.at[a, core, slot, piece(part), lent]
            send(None, ref, z_send.at[a, slot, index, h], z_recv.at[a, slot, part], across[h])

    def hand(a, slot, index):
        part = part_of(index)
        ref = held.at[a, core, slot, piece(part), carried]
        send(None, ref, pass_send.at[a, slot, index], pair_recv.at[a, slot, part], sibling)

    def beside(i):
        for a in (0, 1):
            for way in (0, 1):
                index = ORDER[way][i]
                part = part_of(index)
                ref = held.at[a, core, 1 + way, piece(part), carried]
                arrived(ref, ring_recv.at[a, 1 + way, part])
                if i % 2 == 0:
                    send(
                        ref, held.at[a, core, 3, piece(part), carried],
                        relay_send.at[a, way, i // 2], ring_recv.at[a, 3, part], neighbour[a][way],
                    )
                if index < 2:
                    lend(a, 1 + way, index)
        for a in (0, 1):
            for way in (0, 1):
                hand(a, 1 + way, ORDER[way][i])

    def opposite(index):
        for a in (0, 1):
            part = part_of(index)
            arrived(held.at[a, core, 3, piece(part), carried], ring_recv.at[a, 3, part])
            if index < 2:
                lend(a, 3, index)
        for a in (0, 1):
            hand(a, 3, index)

    def borrowed(slot):
        for h in (0, 1):
            for a in (0, 1):
                for part in (2 * h, 2 * h + 1):
                    arrived(held.at[a, core, slot, piece(part), foreign], z_recv.at[a, slot, part])
                ref = held.at[a, core, slot, piece(2 * h, 2), foreign]
                send(None, ref, zpass_send.at[a, slot, h], zpair_recv.at[a, slot, h], sibling)

    def paired(slot):
        for a in (0, 1):
            for part in range(PARTS):
                arrived(held.at[a, other, slot, piece(part), carried], pair_recv.at[a, slot, part])

    def zpaired(slot):
        for a in (0, 1):
            for h in (0, 1):
                arrived(
                    held.at[a, other, slot, piece(2 * h, 2), foreign], zpair_recv.at[a, slot, h]
                )

    def term(which, half, slot, count, start, width):
        cols = pl.ds(pl.multiple_of(half * HALF + start, 128), width)
        left = weights[which, :, cols]
        right = held[
            0 if which < 2 else 1, half, slot : slot + count, :, pl.ds(pl.multiple_of(start, 128), width)
        ].reshape(count * cap, width)
        return lax.dot_general(left, right, NT, preferred_element_type=jnp.float32)

    def store(which, slot, count, value, add):
        cols = slice(slot * cap, (slot + count) * cap)
        acc[which, :, cols] = acc[which, :, cols] + value if add else value

    def product(which, slot, count):
        value = term(which, 0, slot, count, 0, HALF) + term(which, 1, slot, count, 0, HALF)
        store(which, slot, count, value, False)

    def partial(slot, half, start, width, first=False):
        for which in (0, 1, 2):
            store(which, slot, 1, term(which, half, slot, 1, start, width), not first)

    def slot_of(line, here):
        step = lax.rem(line - here + 4, 4)
        return jnp.where(
            step == 0, 0.0, jnp.where(step == 3, 1.0, jnp.where(step == 1, 2.0, 3.0))
        )

    lane = lax.broadcasted_iota(jnp.int32, (1, 128), 1)
    place_at = lax.broadcasted_iota(jnp.int32, (4 * cap, 128), 0).astype(jnp.float32)
    for s in range(8):
        cols = slice(s * 128, (s + 1) * 128)
        used = info[2, s : s + 1, :] > 0.0
        in_rows = info[0, s : s + 1, :] + slot_of(s // 2, y) * float(cap)
        in_cots = info[1, s : s + 1, :] + slot_of(lax.div(lane, 64) + (s % 2) * 2, x) * float(cap)
        in_rows = jnp.where(used, in_rows, -1.0)
        in_cots = jnp.where(used, in_cots, -1.0)
        row_hot[:, cols] = jnp.where(place_at == in_rows, 1.0, 0.0).astype(jnp.bfloat16)
        cot_hot[:, cols] = jnp.where(place_at == in_cots, 1.0, 0.0).astype(jnp.bfloat16)

    beside(0)

    @pl.loop(0, 4 * cap // 128)
    def _(i):
        some = pl.ds(pl.multiple_of(i * 128, 128), 128)
        perm[some, :] = lax.dot_general(
            cot_hot[some, :], row_hot[...], NT, preferred_element_type=jnp.float32
        ).astype(jnp.bfloat16)

    beside(1)

    def finish(slot, count):
        cols = slice(slot * cap, (slot + count) * cap)
        up = acc[1, :, cols]
        active, slope = gelu_pair(acc[0, :, cols])
        acc[0, :, cols] = active
        acc[1, :, cols] = up * slope
        row_hot[0:HID, cols] = (active * up).astype(jnp.bfloat16)

    def spread(slot, count):
        some = slice(slot * cap, (slot + count) * cap)
        term = acc[2, :, some]
        upper = term.astype(jnp.bfloat16)
        lower = (term - upper.astype(jnp.float32)).astype(jnp.bfloat16)
        for i in range(4 * cap // 256):
            cols = slice(i * 256, (i + 1) * 256)
            moved = jnp.dot(upper, perm[some, cols], preferred_element_type=jnp.float32) + jnp.dot(
                lower, perm[some, cols], preferred_element_type=jnp.float32
            )
            back[:, cols] = moved if slot == 0 else back[:, cols] + moved

    def results(slot, count):
        return [
            pltpu.make_async_copy(
                held.at[a, role, pl.ds(slot, count)],
                out.at[pl.ds(slot, count)],
                result_sem.at[a, slot // 3],
            )
            for a, out in ((0, out_rows), (1, out_cots))
        ]

    for copy in local:
        copy.wait()
    for a in (0, 1):
        for part in range(PARTS):
            arrived(held.at[a, other, 0, piece(part)], pair_recv.at[a, 0, part])
    for which in range(3):
        product(which, 0, 1)
    beside(2)
    beside(3)
    finish(0, 1)
    opposite(0)
    opposite(1)
    spread(0, 1)
    for slot in (1, 2):
        borrowed(slot)
    for slot in (1, 2):
        paired(slot)
    for slot in (1, 2):
        zpaired(slot)
    for copy in results(0, 3):
        copy.start()
    product(0, 1, 2)
    product(1, 1, 2)
    opposite(2)
    opposite(3)
    product(2, 1, 2)
    finish(1, 2)
    borrowed(3)
    spread(1, 2)
    partial(3, core, role * EDGE, WIDE, True)
    partial(3, core, (1 - role) * WIDE, EDGE)
    paired(3)
    partial(3, other, role * EDGE, WIDE)
    zpaired(3)
    for copy in results(3, 1):
        copy.start()
    partial(3, other, (1 - role) * WIDE, EDGE)
    finish(3, 1)
    spread(3, 1)
    for i in range(4 * cap // 128):
        cols = slice(i * 128, (i + 1) * 128)
        staged[1, :, cols] = (back[:, cols] * acc[0, :, cols]).astype(jnp.bfloat16)
        staged[0, :, cols] = (back[:, cols] * acc[1, :, cols]).astype(jnp.bfloat16)
    first = pltpu.make_async_copy(
        staged.at[pl.ds(0, 2)], deltas.at[pl.ds(0, 2)], local_sem.at[0]
    )
    first.start()
    for i in range(4 * cap // 256):
        cols = slice(i * 256, (i + 1) * 256)
        staged[2, :, cols] = lax.dot_general(
            row_hot[0:HID, 0 : 4 * cap], perm[cols, :], NT, preferred_element_type=jnp.float32
        ).astype(jnp.bfloat16)
    second = pltpu.make_async_copy(staged.at[2], deltas.at[2], local_sem.at[1])
    second.start()
    first.wait()
    second.wait()

    for copy in copies:
        copy.wait_send()
    for copy in results(0, 3) + results(3, 1):
        copy.wait()


def forward(cap, packed_rows, packed_cots, info, w_gate, w_up, w_down):
    vmem = pl.BlockSpec(memory_space=pltpu.VMEM)
    hbm = pl.BlockSpec(memory_space=pltpu.HBM)
    small = jax.ShapeDtypeStruct((3, HID, 4 * cap), jnp.bfloat16)
    large = jax.ShapeDtypeStruct((4, cap, HALF), jnp.bfloat16)
    deltas, rows, cots = pl.pallas_call(
        functools.partial(forward_kernel, cap),
        out_shape=(small, large, large),
        in_specs=[hbm, hbm, vmem, hbm, hbm, hbm],
        out_specs=(hbm, hbm, hbm),
        scratch_shapes=[
            pltpu.VMEM((2, 2, 4, cap, HALF), jnp.bfloat16),
            pltpu.VMEM((3, HID, D), jnp.bfloat16),
            pltpu.VMEM((3, HID, 4 * cap), jnp.float32),
            pltpu.VMEM((HID, 4 * cap), jnp.float32),
            pltpu.VMEM((3, HID, 4 * cap), jnp.bfloat16),
            pltpu.VMEM((4 * cap, 1024), jnp.bfloat16),
            pltpu.VMEM((4 * cap, 1024), jnp.bfloat16),
            pltpu.VMEM((4 * cap, 4 * cap), jnp.bfloat16),
            pltpu.SemaphoreType.DMA((2, 3, 4)),
            pltpu.SemaphoreType.DMA((2, 2, 2)),
            pltpu.SemaphoreType.DMA((2, 4, 4)),
            pltpu.SemaphoreType.DMA((2, 4, 2, 2)),
            pltpu.SemaphoreType.DMA((2, 4, 2)),
            pltpu.SemaphoreType.DMA((2, 4, 4)),
            pltpu.SemaphoreType.DMA((2, 4, 4)),
            pltpu.SemaphoreType.DMA((2, 4, 4)),
            pltpu.SemaphoreType.DMA((2, 4, 2)),
            pltpu.SemaphoreType.DMA((5,)),
            pltpu.SemaphoreType.DMA((2, 2)),
        ],
        compiler_params=pltpu.CompilerParams(
            collective_id=2 if cap == 128 else 3,
            has_side_effects=True,
            vmem_limit_bytes=62 * 1024 * 1024,
        ),
    )(packed_rows, packed_cots, info, w_gate, w_up, w_down)
    rows = rows.reshape(4 * cap, HALF)
    cots = cots.reshape(4 * cap, HALF)
    tile = 896
    whole = pl.BlockSpec((3, HID, 4 * cap), lambda i: (0, 0, 0))
    tall = pl.BlockSpec((4 * cap, tile), lambda i: (0, i))
    wide = pl.BlockSpec((HID, tile), lambda i: (0, i))
    return pl.pallas_call(
        gradient_kernel,
        grid=(HALF // tile,),
        out_shape=(jax.ShapeDtypeStruct((HID, HALF), jnp.bfloat16),) * 3,
        in_specs=[whole, tall, tall],
        out_specs=(wide, wide, wide),
        compiler_params=pltpu.CompilerParams(vmem_limit_bytes=62 * 1024 * 1024),
    )(deltas, rows, cots)


def gradient_kernel(deltas, rows, cots, grad_gate, grad_up, grad_down):
    for g, (right, out) in enumerate(((rows, grad_gate), (rows, grad_up), (cots, grad_down))):
        out[...] = jnp.dot(deltas[g], right[...], preferred_element_type=jnp.float32).astype(
            jnp.bfloat16
        )


def local(
    queries, new_keys, new_values, cache_keys, cache_values, context_lengths,
    rollout_rows, cotangents, rewards, prompt_keys, completion_lengths, finished_counts,
    gate_weight, up_weight, down_weight,
):
    attended, packed_rows, packed_cots, info = pack(
        finished_counts, rewards, prompt_keys, completion_lengths, context_lengths,
        rollout_rows, cotangents, queries, new_keys, new_values, cache_keys, cache_values,
    )
    operands = (packed_rows, packed_cots, info, gate_weight.T, up_weight.T, down_weight)
    grad_gate, grad_up, grad_down = lax.cond(
        info[3, 0, 0] <= 128.0,
        functools.partial(forward, 128),
        functools.partial(forward, 256),
        *operands,
    )
    return (attended, grad_gate.T, grad_up.T, grad_down)


def solution(mesh):
    return jax.shard_map(
        local,
        mesh=mesh,
        in_specs=(
            P("fsdp", None, None),
            P("fsdp", None, None),
            P("fsdp", None, None),
            P("fsdp", None, None),
            P("fsdp", None, None),
            P("fsdp"),
            P(("role", "fsdp"), None, None),
            P(("role", "fsdp"), None, None),
            P(("role", "fsdp")),
            P(("role", "fsdp")),
            P(("role", "fsdp")),
            P(("role", "fsdp")),
            P(None, "fsdp"),
            P(None, "fsdp"),
            P("fsdp", None),
        ),
        out_specs=(P("fsdp", None, None), P("role", "fsdp"), P("role", "fsdp"), P("fsdp", "role")),
        check_vma=False,
    )
```

```python
import functools

import jax
import jax.numpy as jnp
from jax import lax
from jax.experimental import pallas as pl
from jax.experimental.pallas import tpu as pltpu
from jax.sharding import PartitionSpec as P

HEADS = 32
KV_HEADS = 16
HEAD_DIM = 128
QSCALAR = 168
GROUP = 16
GROUPS = 8
CL = 256
D = 5376
HALF = 2688
HID = 336
TOK = 16
MESH = pl.DeviceIdType.MESH
NT = (((1,), (1,)), ((), ()))


def gelu_pair(values):
    inner_arg = 0.7978845608028654 * (values + 0.044715 * values * values * values)
    tangent = jnp.tanh(inner_arg)
    result = 0.5 * values * (1.0 + tangent)
    slope_value = 0.5 * (1.0 + tangent) + 0.5 * values * (
        1.0 - tangent * tangent
    ) * 0.7978845608028654 * (1.0 + 3.0 * 0.044715 * values * values)
    return (result, slope_value)


def attend_sample(s, valid, query, fresh_key, fresh_value, keys, values, out, scores, probs, mixed):
    scale = float(QSCALAR) ** (-0.5)

    def stack(ref, count):
        wide = ref[s].astype(jnp.float32)
        parts = [wide[:, j * HEAD_DIM : (j + 1) * HEAD_DIM] for j in range(count)]
        return jnp.concatenate(parts, axis=0)

    asked = stack(query, HEADS)
    new_keys = stack(fresh_key, KV_HEADS).astype(jnp.bfloat16)
    new_values = stack(fresh_value, KV_HEADS).astype(jnp.bfloat16)
    for k in range(KV_HEADS):
        scores[4 * k : 4 * k + 4, :] = lax.dot_general(
            asked[4 * k : 4 * k + 4].astype(jnp.bfloat16),
            keys[s, :, k * HEAD_DIM : (k + 1) * HEAD_DIM],
            NT,
            preferred_element_type=jnp.float32,
        )
    fresh = lax.dot_general(
        asked.astype(jnp.bfloat16), new_keys, NT, preferred_element_type=jnp.float32
    )
    row = lax.broadcasted_iota(jnp.int32, (64, 32), 0)
    column = lax.broadcasted_iota(jnp.int32, (64, 32), 1)
    seen = (lax.div(row, 4) == lax.div(column, 2)) & (lax.rem(column, 2) <= lax.rem(row, 2))
    fresh = jnp.where(seen, fresh * scale, -1e30)
    position = lax.broadcasted_iota(jnp.int32, (64, CL), 1)
    cached = jnp.where(position < valid, scores[...] * scale, -1e30)
    top = jnp.maximum(
        jnp.max(cached, axis=-1, keepdims=True), jnp.max(fresh, axis=-1, keepdims=True)
    )
    cached = jnp.exp(cached - top)
    fresh = jnp.exp(fresh - top)
    total = jnp.sum(cached, axis=-1, keepdims=True) + jnp.sum(fresh, axis=-1, keepdims=True)
    probs[...] = cached / total
    fresh = (fresh / total).astype(jnp.bfloat16)
    mixed[...] = jnp.dot(fresh, new_values, preferred_element_type=jnp.float32)
    for k in range(KV_HEADS):
        mixed[4 * k : 4 * k + 4, :] += jnp.dot(
            probs[4 * k : 4 * k + 4, :].astype(jnp.bfloat16),
            values[s, :, k * HEAD_DIM : (k + 1) * HEAD_DIM],
            preferred_element_type=jnp.float32,
        )
    done = mixed[...]
    out[s] = jnp.concatenate(
        [done[2 * j : 2 * j + 2] for j in range(HEADS)], axis=1
    ).astype(jnp.bfloat16)


def place():
    role = lax.axis_index("role")
    index = lax.axis_index("fsdp")
    return (
        role,
        lax.div(index, 32),
        lax.rem(lax.div(index, 8), 4),
        lax.rem(lax.div(index, 2), 4),
        lax.rem(index, 2),
    )


def device(role, high, x, y, core):
    return {"role": role, "fsdp": ((high * 4 + x) * 4 + y) * 2 + core}


def flip(bit, other):
    return lax.rem(bit + other, 2)


def turn(pos, step):
    return lax.rem(pos + step, 4)


def meet(partners):
    barrier = pltpu.get_barrier_semaphore()
    for partner in partners:
        pl.semaphore_signal(barrier, inc=1, device_id=partner, device_id_type=MESH)
    pl.semaphore_wait(barrier, len(partners))


def remote(src, dst, send, recv, target):
    return pltpu.make_async_remote_copy(
        src_ref=src,
        dst_ref=dst,
        send_sem=send,
        recv_sem=recv,
        device_id=target,
        device_id_type=MESH,
    )


def pack_kernel(
    count_in, reward_in, key_in, length_in, context_in, rows_in, cots_in,
    query_in, fresh_key_in, fresh_value_in, keys_in, values_in,
    attended, out_rows, out_cots, info,
    count, reward, key, length, context, rows, cots, query, fresh_key, fresh_value,
    keys, values, scores, probs, mixed, load_sem, cache_sem,
    src, got, meta, token, col_send, ring_send, data_recv,
    mcol_recv, mx_send, mx_recv, my_send, my_recv,
):
    role, high, x, y, core = place()
    mine = high * 2 + core
    pos = (x, y)
    offsets = [(dr, dh, dc) for dr in (0, 1) for dh in (0, 1) for dc in (0, 1)][1:]
    column = [
        device(flip(role, dr), flip(high, dh), x, y, flip(core, dc)) for dr, dh, dc in offsets
    ]
    x_line = [device(role, high, turn(x, s), y, core) for s in (1, 2, 3)]
    y_line = [device(role, high, x, turn(y, s), core) for s in (1, 2, 3)]
    line = (x_line, y_line)
    neighbour = ((x_line[0], x_line[2]), (y_line[0], y_line[2]))
    loads = [
        pltpu.make_async_copy(a, b, load_sem.at[i])
        for i, (a, b) in enumerate(
            (
                (count_in, count), (reward_in, reward), (key_in, key), (length_in, length),
                (rows_in, rows), (cots_in, cots), (context_in, context), (query_in, query),
                (fresh_key_in, fresh_key), (fresh_value_in, fresh_value),
            )
        )
    ]
    caches = [
        [
            pltpu.make_async_copy(a.at[s], b.at[s], cache_sem.at[s, i])
            for i, (a, b) in enumerate(((keys_in, keys), (values_in, values)))
        ]
        for s in range(4)
    ]
    for copy in loads:
        copy.start()

    def attend(s):
        for copy in caches[s]:
            copy.wait()
        attend_sample(
            s, context[s], query, fresh_key, fresh_value, keys, values, attended,
            scores, probs, mixed,
        )

    for copy in loads[:6]:
        copy.wait()
    meet(column + x_line + y_line)

    copies = []

    def send(src_ref, dst_ref, send_sem, recv_sem, target):
        copy = remote(src_ref, dst_ref, send_sem, recv_sem, target)
        copy.start()
        return copy

    def arrived(ref, sem):
        remote(ref, ref, sem, sem, x_line[0]).wait_recv()

    def column_copies():
        made = []
        for i, (dr, dh, dc) in enumerate(offsets):
            made.append(
                remote(
                    meta.at[y, x, mine], meta.at[y, x, mine],
                    col_send.at[i, 2], mcol_recv.at[mine], column[i],
                )
            )
        for step in (0, 1):
            for i, (dr, dh, dc) in enumerate(offsets):
                if dr == 0 and dh == 1:
                    continue
                part = flip(core, dc)
                a = flip(high, dh + step)
                spot = jnp.where(a == 0, x, y)
                made.append(
                    remote(
                        src.at[a, part], got.at[a, spot, mine],
                        col_send.at[i, a], data_recv.at[a, spot, mine], column[i],
                    )
                )
        return made

    lane = lax.broadcasted_iota(jnp.int32, (8, 128), 1)
    sub = lax.broadcasted_iota(jnp.int32, (8, 128), 0)

    @pl.when(role == 0)
    def _():
        base = (lax.rem(x, 2) * 4 + mine) * TOK
        tile = jnp.zeros((8, 128), jnp.float32)
        for s in range(4):
            here = (lane >= base + 4 * s) & (lane < base + 4 * s + 4)
            live = jnp.where(s < count[0], 1.0, 0.0)
            value = jnp.where(
                sub == 0,
                reward[s],
                jnp.where(
                    sub == 1,
                    key[s].astype(jnp.float32),
                    jnp.where(
                        sub == 2,
                        length[s].astype(jnp.float32),
                        jnp.where(sub == 3, live, 0.0),
                    ),
                ),
            )
            tile = jnp.where(here, value, tile)
        meta[y, x, mine] = tile
        for a, ref in enumerate((rows, cots)):
            wide = jnp.concatenate(
                [ref[s].astype(jnp.float32) for s in range(4)], axis=0
            ).astype(jnp.bfloat16)
            src[a, 0] = wide[:, :HALF]
            src[a, 1] = wide[:, HALF:]
        for copy in column_copies():
            copy.start()
        for a in (0, 1):
            got[a, pos[a], mine] = src[a, core]

    for pair in caches:
        for copy in pair:
            copy.start()
    for copy in loads[6:]:
        copy.wait()

    blocks = [
        flip(high, dh) * 2 + flip(core, dc) for dh, dc in ((0, 0), (0, 1), (1, 0), (1, 1))
    ]

    def spot_of(a):
        return jnp.where(a == 0, x, y)

    def beside(a, way):
        step = 1 if way == 0 else 3
        return device(
            role, high, jnp.where(a == 0, turn(x, step), x), jnp.where(a == 0, y, turn(y, step)), core
        )

    def handed_on(k):
        block = blocks[k]
        here = got.at[high, spot_of(high), block]
        return remote(
            here, here, col_send.at[k, 0], data_recv.at[high, spot_of(high), block],
            device(0, flip(lax.div(block, 2), 1), x, y, core),
        )

    def from_column(a, k, wait=True, hand=False):
        block = blocks[k]
        here = got.at[a, spot_of(a), block]
        sem = data_recv.at[a, spot_of(a), block]
        if wait:
            arrived(here, sem)
        if hand:
            handed_on(k).start()
        for way in (0, 1):
            remote(here, here, ring_send.at[a, way, k], sem, beside(a, way)).start()

    def relay(a, i):
        for way in (0, 1):
            origin = turn(spot_of(a), 3 if way == 0 else 1)
            block = 2 * flip(high, i) + way
            here = got.at[a, origin, block]
            sem = data_recv.at[a, origin, block]
            arrived(here, sem)
            remote(here, here, ring_send.at[a, way, 4 + i], sem, beside(a, way)).start()

    def wait_column(k, what):
        if k == 0:
            @pl.when(role == 1)
            def _():
                what()
        else:
            what()

    @pl.when(role == 0)
    def _():
        for k in (0, 1):
            for a in (0, 1):
                from_column(a, k, wait=k > 0)

    @pl.when(role == 1)
    def _():
        for k in range(4):
            from_column(high, k, hand=True)

    for k, block in enumerate(blocks):
        wait_column(
            k, lambda block=block: arrived(meta.at[y, x, block], mcol_recv.at[block])
        )
    for i in range(3):
        copies.append(
            send(meta.at[y, x], meta.at[y, x], mx_send.at[i], mx_recv.at[x], x_line[i])
        )

    @pl.when(role == 0)
    def _():
        for a in (0, 1):
            relay(a, 0)
        for k in (2, 3):
            for a in (0, 1):
                from_column(a, k)

    @pl.when(role == 1)
    def _():
        for i in (0, 1):
            for k in (2 * i, 2 * i + 1):
                from_column(1 - high, k)
            relay(high, i)

    for i in (1, 2, 3):
        other = turn(x, i)
        arrived(meta.at[y, other], mx_recv.at[other])
    for i in range(3):
        copies.append(send(meta.at[y], meta.at[y], my_send.at[i], my_recv.at[y], y_line[i]))

    @pl.when(role == 0)
    def _():
        for a in (0, 1):
            relay(a, 1)

    @pl.when(role == 1)
    def _():
        for i in (0, 1):
            relay(1 - high, i)

    attend(0)
    for i in (1, 2, 3):
        other = turn(y, i)
        arrived(meta.at[other], my_recv.at[other])

    attend(1)
    attend(2)
    attend(3)

    tiles = []
    for s in range(8):
        total = jnp.zeros((8, 128), jnp.float32)
        for xi in (0, 1):
            for block in range(4):
                total = total + meta[s // 2, (s % 2) * 2 + xi, block]
        tiles.append(total)
    rewards, keys, lengths, live = (
        jnp.concatenate([t[q : q + 1] for t in tiles], axis=0) for q in range(4)
    )
    step = lax.rem(lane, 4).astype(jnp.float32)
    first = jnp.where(step == 0.0, live, 0.0)
    mean = jnp.zeros((8, 128), jnp.float32)
    denominator = jnp.ones((8, 128), jnp.float32)
    for k in range(GROUPS):
        same = keys == float(k)
        member = jnp.where(same, first, 0.0)
        group_sum = jnp.sum(member * rewards, axis=(0, 1), keepdims=True)
        group_sq = jnp.sum(member * (rewards * rewards), axis=(0, 1), keepdims=True)
        group_mean = group_sum / GROUP
        spread = group_sq / GROUP - group_mean * group_mean
        divisor = jnp.maximum(jnp.sqrt(jnp.maximum(spread, 0.0)), 1.0)
        mean = jnp.where(same, group_mean, mean)
        denominator = jnp.where(same, divisor, denominator)
    used = (live > 0.0) & (step < lengths)
    mask = jnp.where(used, 1.0, 0.0)
    weight = jnp.where(used, (rewards - mean) / denominator / jnp.maximum(lengths, 1.0), 0.0)

    a_lane = lax.broadcasted_iota(jnp.int32, (128, 128), 0)
    b_lane = lax.broadcasted_iota(jnp.int32, (128, 128), 1)
    same_column = (a_lane < 64) == (b_lane < 64)

    def count_by(take):
        return jnp.dot(
            mask.astype(jnp.bfloat16),
            jnp.where(take, 1.0, 0.0).astype(jnp.bfloat16),
            preferred_element_type=jnp.float32,
        )

    before_all = count_by(a_lane < b_lane)
    before_column = count_by((a_lane < b_lane) & same_column)
    whole = jnp.sum(mask, axis=1, keepdims=True) + jnp.zeros((8, 128), jnp.float32)
    own_column = count_by(same_column)
    rank_y_rows, rank_x_rows = [], []
    for s in range(8):
        ry = before_all[s : s + 1]
        if s % 2 == 1:
            ry = ry + whole[s - 1 : s]
        rx = before_column[s : s + 1]
        for t in range(s % 2, s, 2):
            rx = rx + own_column[t : t + 1]
        rank_y_rows.append(ry)
        rank_x_rows.append(rx)
    rank_y = jnp.concatenate(rank_y_rows, axis=0)
    rank_x = jnp.concatenate(rank_x_rows, axis=0)
    load = jnp.zeros((1, 1), jnp.float32)
    for g in range(4):
        in_y = jnp.where(lax.div(sub, 2) == g, mask, 0.0)
        in_x = jnp.where(lax.rem(sub, 2) * 2 + lax.div(lane, 64) == g, mask, 0.0)
        load = jnp.maximum(load, jnp.sum(in_y, axis=(0, 1), keepdims=True))
        load = jnp.maximum(load, jnp.sum(in_x, axis=(0, 1), keepdims=True))
    info[0] = jnp.where(used, rank_y, -1.0)
    info[1] = jnp.where(used, rank_x, -1.0)
    info[2] = mask
    info[3] = load + jnp.zeros((8, 128), jnp.float32)

    token[0] = jnp.where(used, rank_y, -1.0)
    swapped = lax.rem(x, 2) == 1
    for q, value in ((1, jnp.where(used, rank_x, -1.0)), (2, weight)):
        rolled = pltpu.roll(value, 64, 1)
        token[q] = jnp.where(swapped, rolled, value)
        token[q + 2] = jnp.where(swapped, value, rolled)

    def y_row(q):
        return jnp.concatenate(
            [token[q, pl.ds(2 * y, 1), :], token[q, pl.ds(2 * y + 1, 1), :]], axis=1
        )

    def x_row(q):
        low = lax.broadcasted_iota(jnp.int32, (1, 128), 1) < 64
        half_x = lax.div(x, 2)
        parts = [
            jnp.where(
                low,
                token[q, pl.ds(2 * t + half_x, 1), :],
                token[q + 2, pl.ds(2 * t + 2 + half_x, 1), :],
            )
            for t in (0, 2)
        ]
        return jnp.concatenate(parts, axis=1)

    target = lax.broadcasted_iota(jnp.int32, (256, 256), 0).astype(jnp.float32)
    pick_rows = jnp.where(target == y_row(0), 1.0, 0.0).astype(jnp.bfloat16)
    chosen = target == x_row(1)
    pick_cots = jnp.where(chosen, 1.0, 0.0).astype(jnp.bfloat16)
    row_weight = jnp.sum(jnp.where(chosen, x_row(2), 0.0), axis=1, keepdims=True)

    for a in (0, 1):
        for way in (0, 1):
            origin = turn(pos[a], 3 if way == 0 else 1)
            for block in range(4):
                if block % 2 != way:
                    arrived(got.at[a, origin, block], data_recv.at[a, origin, block])
        origin = turn(pos[a], 2)
        for block in range(4):
            arrived(got.at[a, origin, block], data_recv.at[a, origin, block])

    for part in range(7):
        cols = slice(part * 384, (part + 1) * 384)
        block = got[0, :, :, :, cols].reshape(256, 384)
        out_rows[:, cols] = jnp.dot(
            pick_rows, block, preferred_element_type=jnp.float32
        ).astype(jnp.bfloat16)
        block = got[1, :, :, :, cols].reshape(256, 384)
        packed = jnp.dot(pick_cots, block, preferred_element_type=jnp.float32)
        out_cots[:, cols] = (packed * row_weight).astype(jnp.bfloat16)

    for copy in copies:
        copy.wait_send()
    for a in (0, 1):
        for way in (0, 1):
            for k in range(6):
                here = got.at[a, pos[a], mine]
                sem = ring_send.at[a, way, k]
                remote(here, here, sem, sem, beside(a, way)).wait_send()

    @pl.when(role == 0)
    def _():
        for copy in column_copies():
            copy.wait_send()

    @pl.when(role == 1)
    def _():
        for k in range(4):
            handed_on(k).wait_send()


def pack(*operands):
    vmem = pl.BlockSpec(memory_space=pltpu.VMEM)
    queries, new_keys, cache_keys = operands[7], operands[8], operands[10]
    return pl.pallas_call(
        pack_kernel,
        out_shape=(
            jax.ShapeDtypeStruct(queries.shape, jnp.bfloat16),
            jax.ShapeDtypeStruct((256, HALF), jnp.bfloat16),
            jax.ShapeDtypeStruct((256, HALF), jnp.bfloat16),
            jax.ShapeDtypeStruct((4, 8, 128), jnp.float32),
        ),
        in_specs=[pl.BlockSpec(memory_space=pltpu.HBM)] * len(operands),
        out_specs=(vmem, vmem, vmem, vmem),
        scratch_shapes=[
            pltpu.SMEM((1,), jnp.int32),
            pltpu.SMEM((4,), jnp.float32),
            pltpu.SMEM((4,), jnp.int32),
            pltpu.SMEM((4,), jnp.int32),
            pltpu.SMEM((4,), jnp.int32),
            pltpu.VMEM((4, 4, D), jnp.bfloat16),
            pltpu.VMEM((4, 4, D), jnp.bfloat16),
            pltpu.VMEM(queries.shape, jnp.bfloat16),
            pltpu.VMEM(new_keys.shape, jnp.bfloat16),
            pltpu.VMEM(new_keys.shape, jnp.bfloat16),
            pltpu.VMEM(cache_keys.shape, jnp.bfloat16),
            pltpu.VMEM(cache_keys.shape, jnp.bfloat16),
            pltpu.VMEM((64, CL), jnp.float32),
            pltpu.VMEM((64, CL), jnp.float32),
            pltpu.VMEM((64, HEAD_DIM), jnp.float32),
            pltpu.SemaphoreType.DMA((10,)),
            pltpu.SemaphoreType.DMA((4, 2)),
            pltpu.VMEM((2, 2, TOK, HALF), jnp.bfloat16),
            pltpu.VMEM((2, 4, 4, TOK, HALF), jnp.bfloat16),
            pltpu.VMEM((4, 4, 4, 8, 128), jnp.float32),
            pltpu.VMEM((5, 8, 128), jnp.float32),
            pltpu.SemaphoreType.DMA((7, 3)),
            pltpu.SemaphoreType.DMA((2, 2, 6)),
            pltpu.SemaphoreType.DMA((2, 4, 4)),
            pltpu.SemaphoreType.DMA((4,)),
            pltpu.SemaphoreType.DMA((3,)),
            pltpu.SemaphoreType.DMA((4,)),
            pltpu.SemaphoreType.DMA((3,)),
            pltpu.SemaphoreType.DMA((4,)),
        ],
        compiler_params=pltpu.CompilerParams(
            collective_id=1, has_side_effects=True, vmem_limit_bytes=62 * 1024 * 1024
        ),
    )(*operands)


PARTS = 4
EDGE = 896
WIDE = HALF - EDGE
ORDER = ((0, 1, 2, 3), (1, 0, 3, 2))


def forward_kernel(
    cap, packed_rows, packed_cots, info, w_gate, w_up, w_down,
    deltas, out_rows, out_cots,
    held, weights, acc, back, staged, row_hot, cot_hot, perm,
    own_send, relay_send, pass_send, z_send, zpass_send,
    ring_recv, pair_recv, z_recv, zpair_recv, local_sem, result_sem,
):
    role, high, x, y, core = place()
    pos = (y, x)
    rows = cap // PARTS
    other = flip(core, 1)
    sibling = device(role, high, x, y, other)
    neighbour = (
        (device(role, high, x, turn(y, 1), core), device(role, high, x, turn(y, 3), core)),
        (device(role, high, turn(x, 1), y, core), device(role, high, turn(x, 3), y, core)),
    )
    across = [device(flip(role, 1), h, x, y, core) for h in (0, 1)]
    carried = pl.ds(pl.multiple_of(role * EDGE, 128), WIDE)
    lent = pl.ds(pl.multiple_of(role * WIDE, 128), EDGE)
    foreign = pl.ds(pl.multiple_of((1 - role) * WIDE, 128), EDGE)
    source = (packed_rows, packed_cots)
    local = [
        pltpu.make_async_copy(source[a].at[pl.ds(0, cap)], held.at[a, core, 0], local_sem.at[a])
        for a in (0, 1)
    ] + [
        pltpu.make_async_copy(w, weights.at[i], local_sem.at[2 + i])
        for i, w in enumerate((w_gate, w_up, w_down))
    ]
    for copy in local:
        copy.start()
    meet([sibling, *neighbour[0], *neighbour[1], *across])

    copies = []

    def part_of(index):
        return lax.rem(index + 2 * high, PARTS)

    def piece(part, count=1):
        return pl.ds(pl.multiple_of(part * rows, rows), rows * count)

    def send(src, dst, send_sem, recv_sem, target):
        copy = remote(dst if src is None else src, dst, send_sem, recv_sem, target)
        copy.start()
        copies.append(copy)

    def arrived(ref, sem):
        remote(ref, ref, sem, sem, sibling).wait_recv()

    for i in range(PARTS):
        for a in (0, 1):
            for way in (0, 1):
                part = part_of(ORDER[way][i])
                send(
                    source[a].at[piece(part), carried],
                    held.at[a, core, 1 + way, piece(part), carried],
                    own_send.at[a, way, i], ring_recv.at[a, 1 + way, part], neighbour[a][way],
                )
            part = part_of(i)
            send(
                source[a].at[piece(part)], held.at[a, core, 0, piece(part)],
                own_send.at[a, 2, i], pair_recv.at[a, 0, part], sibling,
            )

    def lend(a, slot, index):
        part = part_of(index)
        for h in (0, 1):
            ref = held.at[a, core, slot, piece(part), lent]
            send(None, ref, z_send.at[a, slot, index, h], z_recv.at[a, slot, part], across[h])

    def hand(a, slot, index):
        part = part_of(index)
        ref = held.at[a, core, slot, piece(part), carried]
        send(None, ref, pass_send.at[a, slot, index], pair_recv.at[a, slot, part], sibling)

    def beside(i):
        for a in (0, 1):
            for way in (0, 1):
                index = ORDER[way][i]
                part = part_of(index)
                ref = held.at[a, core, 1 + way, piece(part), carried]
                arrived(ref, ring_recv.at[a, 1 + way, part])
                if i % 2 == 0:
                    send(
                        ref, held.at[a, core, 3, piece(part), carried],
                        relay_send.at[a, way, i // 2], ring_recv.at[a, 3, part], neighbour[a][way],
                    )
                if index < 2:
                    lend(a, 1 + way, index)
        for a in (0, 1):
            for way in (0, 1):
                hand(a, 1 + way, ORDER[way][i])

    def opposite(index):
        for a in (0, 1):
            part = part_of(index)
            arrived(held.at[a, core, 3, piece(part), carried], ring_recv.at[a, 3, part])
            if index < 2:
                lend(a, 3, index)
        for a in (0, 1):
            hand(a, 3, index)

    def borrowed(slot):
        for h in (0, 1):
            for a in (0, 1):
                for part in (2 * h, 2 * h + 1):
                    arrived(held.at[a, core, slot, piece(part), foreign], z_recv.at[a, slot, part])
                ref = held.at[a, core, slot, piece(2 * h, 2), foreign]
                send(None, ref, zpass_send.at[a, slot, h], zpair_recv.at[a, slot, h], sibling)

    def paired(slot):
        for a in (0, 1):
            for part in range(PARTS):
                arrived(held.at[a, other, slot, piece(part), carried], pair_recv.at[a, slot, part])

    def zpaired(slot):
        for a in (0, 1):
            for h in (0, 1):
                arrived(
                    held.at[a, other, slot, piece(2 * h, 2), foreign], zpair_recv.at[a, slot, h]
                )

    def term(which, half, slot, count, start, width):
        cols = pl.ds(pl.multiple_of(half * HALF + start, 128), width)
        left = weights[which, :, cols]
        right = held[
            0 if which < 2 else 1, half, slot : slot + count, :, pl.ds(pl.multiple_of(start, 128), width)
        ].reshape(count * cap, width)
        return lax.dot_general(left, right, NT, preferred_element_type=jnp.float32)

    def store(which, slot, count, value, add):
        cols = slice(slot * cap, (slot + count) * cap)
        acc[which, :, cols] = acc[which, :, cols] + value if add else value

    def product(which, slot, count):
        value = term(which, 0, slot, count, 0, HALF) + term(which, 1, slot, count, 0, HALF)
        store(which, slot, count, value, False)

    def partial(slot, half, start, width, first=False):
        for which in (0, 1, 2):
            store(which, slot, 1, term(which, half, slot, 1, start, width), not first)

    def slot_of(line, here):
        step = lax.rem(line - here + 4, 4)
        return jnp.where(
            step == 0, 0.0, jnp.where(step == 3, 1.0, jnp.where(step == 1, 2.0, 3.0))
        )

    lane = lax.broadcasted_iota(jnp.int32, (1, 128), 1)
    place_at = lax.broadcasted_iota(jnp.int32, (4 * cap, 128), 0).astype(jnp.float32)
    for s in range(8):
        cols = slice(s * 128, (s + 1) * 128)
        used = info[2, s : s + 1, :] > 0.0
        in_rows = info[0, s : s + 1, :] + slot_of(s // 2, y) * float(cap)
        in_cots = info[1, s : s + 1, :] + slot_of(lax.div(lane, 64) + (s % 2) * 2, x) * float(cap)
        in_rows = jnp.where(used, in_rows, -1.0)
        in_cots = jnp.where(used, in_cots, -1.0)
        row_hot[:, cols] = jnp.where(place_at == in_rows, 1.0, 0.0).astype(jnp.bfloat16)
        cot_hot[:, cols] = jnp.where(place_at == in_cots, 1.0, 0.0).astype(jnp.bfloat16)

    beside(0)

    @pl.loop(0, 4 * cap // 128)
    def _(i):
        some = pl.ds(pl.multiple_of(i * 128, 128), 128)
        perm[some, :] = lax.dot_general(
            cot_hot[some, :], row_hot[...], NT, preferred_element_type=jnp.float32
        ).astype(jnp.bfloat16)

    beside(1)

    def finish(slot, count):
        cols = slice(slot * cap, (slot + count) * cap)
        up = acc[1, :, cols]
        active, slope = gelu_pair(acc[0, :, cols])
        acc[0, :, cols] = active
        acc[1, :, cols] = up * slope
        row_hot[0:HID, cols] = (active * up).astype(jnp.bfloat16)

    def spread(slot, count):
        some = slice(slot * cap, (slot + count) * cap)
        term = acc[2, :, some]
        upper = term.astype(jnp.bfloat16)
        lower = (term - upper.astype(jnp.float32)).astype(jnp.bfloat16)
        for i in range(4 * cap // 256):
            cols = slice(i * 256, (i + 1) * 256)
            moved = jnp.dot(upper, perm[some, cols], preferred_element_type=jnp.float32) + jnp.dot(
                lower, perm[some, cols], preferred_element_type=jnp.float32
            )
            back[:, cols] = moved if slot == 0 else back[:, cols] + moved

    def results(slot, count):
        return [
            pltpu.make_async_copy(
                held.at[a, role, pl.ds(slot, count)],
                out.at[pl.ds(slot, count)],
                result_sem.at[a, slot // 3],
            )
            for a, out in ((0, out_rows), (1, out_cots))
        ]

    for copy in local:
        copy.wait()
    for a in (0, 1):
        for part in range(PARTS):
            arrived(held.at[a, other, 0, piece(part)], pair_recv.at[a, 0, part])
    for which in range(3):
        product(which, 0, 1)
    beside(2)
    beside(3)
    finish(0, 1)
    opposite(0)
    opposite(1)
    spread(0, 1)
    for slot in (1, 2):
        borrowed(slot)
    for slot in (1, 2):
        paired(slot)
    for slot in (1, 2):
        zpaired(slot)
    for copy in results(0, 3):
        copy.start()
    product(0, 1, 2)
    product(1, 1, 2)
    opposite(2)
    opposite(3)
    product(2, 1, 2)
    finish(1, 2)
    spread(1, 2)
    partial(3, core, role * EDGE, WIDE, True)
    borrowed(3)
    paired(3)
    partial(3, other, role * EDGE, WIDE)
    partial(3, core, (1 - role) * WIDE, EDGE)
    zpaired(3)
    for copy in results(3, 1):
        copy.start()
    partial(3, other, (1 - role) * WIDE, EDGE)
    finish(3, 1)
    spread(3, 1)
    for i in range(4 * cap // 128):
        cols = slice(i * 128, (i + 1) * 128)
        staged[1, :, cols] = (back[:, cols] * acc[0, :, cols]).astype(jnp.bfloat16)
        staged[0, :, cols] = (back[:, cols] * acc[1, :, cols]).astype(jnp.bfloat16)
    first = pltpu.make_async_copy(
        staged.at[pl.ds(0, 2)], deltas.at[pl.ds(0, 2)], local_sem.at[0]
    )
    first.start()
    for i in range(4 * cap // 256):
        cols = slice(i * 256, (i + 1) * 256)
        staged[2, :, cols] = lax.dot_general(
            row_hot[0:HID, 0 : 4 * cap], perm[cols, :], NT, preferred_element_type=jnp.float32
        ).astype(jnp.bfloat16)
    second = pltpu.make_async_copy(staged.at[2], deltas.at[2], local_sem.at[1])
    second.start()
    first.wait()
    second.wait()

    for copy in copies:
        copy.wait_send()
    for copy in results(0, 3) + results(3, 1):
        copy.wait()


def forward(cap, packed_rows, packed_cots, info, w_gate, w_up, w_down):
    vmem = pl.BlockSpec(memory_space=pltpu.VMEM)
    hbm = pl.BlockSpec(memory_space=pltpu.HBM)
    small = jax.ShapeDtypeStruct((3, HID, 4 * cap), jnp.bfloat16)
    large = jax.ShapeDtypeStruct((4, cap, HALF), jnp.bfloat16)
    deltas, rows, cots = pl.pallas_call(
        functools.partial(forward_kernel, cap),
        out_shape=(small, large, large),
        in_specs=[hbm, hbm, vmem, hbm, hbm, hbm],
        out_specs=(hbm, hbm, hbm),
        scratch_shapes=[
            pltpu.VMEM((2, 2, 4, cap, HALF), jnp.bfloat16),
            pltpu.VMEM((3, HID, D), jnp.bfloat16),
            pltpu.VMEM((3, HID, 4 * cap), jnp.float32),
            pltpu.VMEM((HID, 4 * cap), jnp.float32),
            pltpu.VMEM((3, HID, 4 * cap), jnp.bfloat16),
            pltpu.VMEM((4 * cap, 1024), jnp.bfloat16),
            pltpu.VMEM((4 * cap, 1024), jnp.bfloat16),
            pltpu.VMEM((4 * cap, 4 * cap), jnp.bfloat16),
            pltpu.SemaphoreType.DMA((2, 3, 4)),
            pltpu.SemaphoreType.DMA((2, 2, 2)),
            pltpu.SemaphoreType.DMA((2, 4, 4)),
            pltpu.SemaphoreType.DMA((2, 4, 2, 2)),
            pltpu.SemaphoreType.DMA((2, 4, 2)),
            pltpu.SemaphoreType.DMA((2, 4, 4)),
            pltpu.SemaphoreType.DMA((2, 4, 4)),
            pltpu.SemaphoreType.DMA((2, 4, 4)),
            pltpu.SemaphoreType.DMA((2, 4, 2)),
            pltpu.SemaphoreType.DMA((5,)),
            pltpu.SemaphoreType.DMA((2, 2)),
        ],
        compiler_params=pltpu.CompilerParams(
            collective_id=2 if cap == 128 else 3,
            has_side_effects=True,
            vmem_limit_bytes=62 * 1024 * 1024,
        ),
    )(packed_rows, packed_cots, info, w_gate, w_up, w_down)
    rows = rows.reshape(4 * cap, HALF)
    cots = cots.reshape(4 * cap, HALF)
    tile = 896
    whole = pl.BlockSpec((3, HID, 4 * cap), lambda i: (0, 0, 0))
    tall = pl.BlockSpec((4 * cap, tile), lambda i: (0, i))
    wide = pl.BlockSpec((HID, tile), lambda i: (0, i))
    return pl.pallas_call(
        gradient_kernel,
        grid=(HALF // tile,),
        out_shape=(jax.ShapeDtypeStruct((HID, HALF), jnp.bfloat16),) * 3,
        in_specs=[whole, tall, tall],
        out_specs=(wide, wide, wide),
        compiler_params=pltpu.CompilerParams(vmem_limit_bytes=62 * 1024 * 1024),
    )(deltas, rows, cots)


def gradient_kernel(deltas, rows, cots, grad_gate, grad_up, grad_down):
    for g, (right, out) in enumerate(((rows, grad_gate), (rows, grad_up), (cots, grad_down))):
        out[...] = jnp.dot(deltas[g], right[...], preferred_element_type=jnp.float32).astype(
            jnp.bfloat16
        )


def local(
    queries, new_keys, new_values, cache_keys, cache_values, context_lengths,
    rollout_rows, cotangents, rewards, prompt_keys, completion_lengths, finished_counts,
    gate_weight, up_weight, down_weight,
):
    attended, packed_rows, packed_cots, info = pack(
        finished_counts, rewards, prompt_keys, completion_lengths, context_lengths,
        rollout_rows, cotangents, queries, new_keys, new_values, cache_keys, cache_values,
    )
    operands = (packed_rows, packed_cots, info, gate_weight.T, up_weight.T, down_weight)
    grad_gate, grad_up, grad_down = lax.cond(
        info[3, 0, 0] <= 128.0,
        functools.partial(forward, 128),
        functools.partial(forward, 256),
        *operands,
    )
    return (attended, grad_gate.T, grad_up.T, grad_down)


def solution(mesh):
    return jax.shard_map(
        local,
        mesh=mesh,
        in_specs=(
            P("fsdp", None, None),
            P("fsdp", None, None),
            P("fsdp", None, None),
            P("fsdp", None, None),
            P("fsdp", None, None),
            P("fsdp"),
            P(("role", "fsdp"), None, None),
            P(("role", "fsdp"), None, None),
            P(("role", "fsdp")),
            P(("role", "fsdp")),
            P(("role", "fsdp")),
            P(("role", "fsdp")),
            P(None, "fsdp"),
            P(None, "fsdp"),
            P("fsdp", None),
        ),
        out_specs=(P("fsdp", None, None), P("role", "fsdp"), P("role", "fsdp"), P("fsdp", "role")),
        check_vma=False,
    )
```
